256 devices in a mesh: replica: 16 (over y, x_lo, core), fsdp: 16 (over z, x_hi).
Axes of the slice: x: 4 (x_hi: 2, x_lo: 2; x = x_hi * 2 + x_lo), y: 4, z: 8, core: 2. Of those that a mesh axis runs over, the one named last changes fastest.
Arguments:
- hidden_in: bfloat16 [16, 4096, 3584], P('replica', 'fsdp'), may hold values from -6 to 6
- local_weights: bfloat16 [16, 3584, 2048], P('replica', 'fsdp'), may hold values from -6 to 6
- cotangent: bfloat16 [16, 4096, 2048], P('replica', 'fsdp'), may hold values from -6 to 6
- global_weights: float32 [3584, 2048], P('fsdp'), may hold values from -6 to 6
- outer_momentum: float32 [3584, 2048], P('fsdp'), may hold values from -3 to 3
- step_index: int32 [1], replicated, may hold values from 0 to 1023
Outputs:
- projected: bfloat16 [16, 4096, 2048], P('replica', 'fsdp')
- input_grad: bfloat16 [16, 4096, 3584], P('replica', 'fsdp')
- new_weights: bfloat16 [16, 3584, 2048], P('replica', 'fsdp')
- new_global: float32 [3584, 512], P('fsdp')
- new_momentum: float32 [3584, 512], P('fsdp')
The draws below stay inside these ranges and needn't reach their ends.
All inputs are finite; a program needn't handle non-finite values.
Results may differ from the reference program's by a relative error of at most 0.013.
Values may be sent and summed in bfloat16 or wider, within the bound.
A program may use at most 128 MiB of HBM per device.

```python
import math
import jax
import jax.numpy as jnp
from jax import lax

DW = 3584
KVW = 2048
FRAGS = 4
FRAGW = 512
TOK_DEV = 256
TOKENS = 4096
NREP = 16
N_FSDP = 16


def levels(stream_key, dims, cuts, least, high):
    level = 1.0
    for dim, shards_of in cuts:
        heights = jax.random.uniform(jax.random.fold_in(jax.random.fold_in(stream_key, 6), dim), (shards_of,), jnp.float32, least / len(cuts), high / len(cuts))
        level = level * jnp.repeat(jnp.exp(heights), dims[dim] // shards_of).reshape((-1,) + (1,) * (len(dims) - 1 - dim))
    return level


def noise(stream_key, shape, spread, reach, cuts=(), kind=jnp.bfloat16):
    values = jax.random.normal(stream_key, shape, jnp.float32) * spread
    if len(cuts) > 0:
        values = levels(stream_key, shape, cuts, -0.22, 0.18) * values
    return jnp.clip(values, min=-reach, max=reach).astype(kind)


def setup_inputs(seed: int = 0) -> dict:
    keys = jax.random.split(jax.random.key(seed), 7)
    hidden_in = noise(keys[0], (NREP, TOKENS, DW), 1.0, 6.0, ((0, 16), (1, 16)))
    local_weights = noise(keys[1], (NREP, DW, KVW), 1.0, 6.0, ((0, 16), (1, 16)))
    cotangent = noise(keys[2], (NREP, TOKENS, KVW), 1.0, 6.0, ((0, 16), (1, 16)))
    global_weights = noise(keys[3], (DW, KVW), 1.0, 6.0, ((0, 16),), jnp.float32)
    outer_momentum = noise(keys[4], (DW, KVW), 0.5, 3.0, ((0, 16),), jnp.float32)
    step_index = jax.random.randint(keys[5], (1,), 0, 1024).astype(jnp.int32)
    return {"hidden_in": hidden_in, "local_weights": local_weights, "cotangent": cotangent, "global_weights": global_weights, "outer_momentum": outer_momentum, "step_index": step_index}


EPSILON = 1e-05
INNER_RATE = 0.25
OUTER_RATE = 0.7
NESTEROV = 0.9
MIX_KEEP = 0.5

def replica_step(pieces):
    hidden_in, weights, cotangent = pieces
    scale = 1.0 / math.sqrt(DW)
    wide = hidden_in.astype(jnp.float32)
    rms = jnp.sqrt(lax.optimization_barrier(jnp.mean(wide * wide, -1, keepdims=True)) + EPSILON)
    exact = wide / rms
    normed = exact.astype(jnp.bfloat16)
    projected = (jnp.dot(normed, weights, preferred_element_type=jnp.float32) * scale).astype(jnp.bfloat16)
    back = lax.dot_general(cotangent, weights, (((1,), (1,)), ((), ())), preferred_element_type=jnp.float32) * scale
    input_grad = ((back - exact * lax.optimization_barrier(jnp.mean(back * exact, -1, keepdims=True))) / rms).astype(jnp.bfloat16)
    blocks_n = normed.reshape(N_FSDP, TOK_DEV, DW).astype(jnp.float32)
    blocks_d = cotangent.reshape(N_FSDP, TOK_DEV, KVW).astype(jnp.float32)
    partial_terms = (jnp.einsum('ftd,ftk->fdk', blocks_n, blocks_d) * scale).astype(jnp.bfloat16).astype(jnp.float32)
    gradient = lax.optimization_barrier(jnp.sum(partial_terms, 0))
    updated = weights.astype(jnp.float32) - INNER_RATE * gradient
    return (projected, input_grad, updated)

def reference(hidden_in, local_weights, cotangent, global_weights, outer_momentum, step_index):
    projected, input_grad, updated = lax.map(replica_step, (hidden_in, local_weights, cotangent))
    start = (step_index[0] % FRAGS * FRAGW).astype(jnp.int32)
    local_frag = lax.dynamic_slice_in_dim(local_weights.astype(jnp.float32), start, FRAGW, 2)
    mean_frag = lax.optimization_barrier(jnp.sum(local_frag, 0)) / NREP
    global_frag = lax.dynamic_slice_in_dim(global_weights, start, FRAGW, 1)
    moment_frag = lax.dynamic_slice_in_dim(outer_momentum, start, FRAGW, 1)
    delta = global_frag - mean_frag
    new_momentum = NESTEROV * moment_frag + delta
    new_global = global_frag - OUTER_RATE * (delta + NESTEROV * new_momentum)
    upd_frag = lax.dynamic_slice_in_dim(updated, start, FRAGW, 2)
    mixed = MIX_KEEP * upd_frag + (1.0 - MIX_KEEP) * new_global[None]
    new_weights = lax.dynamic_update_slice_in_dim(updated, mixed, start, 2).astype(jnp.bfloat16)
    return (projected, input_grad, new_weights, new_global, new_momentum)
```

```python
import functools
import math

import jax
import jax.numpy as jnp
from jax import lax
from jax.experimental import pallas as pl
from jax.experimental.pallas import tpu as pltpu
from jax.sharding import PartitionSpec as P

KVW = 2048
FRAGS = 4
DW = 3584
HALF = DW // 2
TOK = 256
ROWS = 224
SIDE = ROWS // 2
NZ = 8
PARTS = 2
WIDE = KVW // PARTS
SCALE = 1.0 / math.sqrt(DW)

EPSILON = 1e-05
INNER_RATE = 0.25
OUTER_RATE = 0.7
NESTEROV = 0.9
MIX_KEEP = 0.5

MESH = pl.DeviceIdType.MESH
F32 = jnp.float32
BF16 = jnp.bfloat16


def outer_update(global_part, moment_part, mean_part):
    delta = global_part - mean_part
    moment_next = NESTEROV * moment_part + delta
    global_next = global_part - OUTER_RATE * (delta + NESTEROV * moment_next)
    return (global_next, moment_next)


def dot_nn(a, b):
    return jnp.dot(a, b, preferred_element_type=F32)


def dot_nt(a, b):
    return lax.dot_general(a, b, (((1,), (1,)), ((), ())), preferred_element_type=F32)


def chunk(i, size):
    return pl.ds(pl.multiple_of(i * size, size), size)


def kernel(
    hid_in, w_in, g_in, proj_out, ig_out, grad_out,
    hid, g_own, g_far, ht, n_halves, n_far, n_rows, wg, grads, ring,
    back_own, back_send, back_far, p_own, p_send, p_far, igt, ig_rows, p_rows,
    ag_send, ag_recv, rs_send, rs_recv, x_send, x_recv, local,
):
    replica = lax.axis_index("replica")
    place = lax.axis_index("fsdp")
    z, side = place // 2, lax.rem(place, 2)
    up = (replica, lax.rem(z + 1, NZ) * 2 + side)
    down = (replica, lax.rem(z + NZ - 1, NZ) * 2 + side)
    partner = (replica, z * 2 + 1 - side)

    def half_rows(block, d):
        return pl.ds(pl.multiple_of(block * ROWS + d * SIDE, 16), SIDE)

    def ring_block(step, d):
        return lax.rem(z - step + 2 * NZ, NZ) if d == 0 else lax.rem(z + step, NZ)

    load_hid = pltpu.make_async_copy(hid_in, hid, local.at[0])
    load_g = pltpu.make_async_copy(g_in, g_own, local.at[1])
    load_w = pltpu.make_async_copy(
        w_in, wg.at[pl.ds(pl.multiple_of(z * ROWS, 16), ROWS)], local.at[2]
    )
    load_hid.start()
    load_g.start()
    load_w.start()

    barrier = pltpu.get_barrier_semaphore()
    for other in (up, down, partner):
        pl.semaphore_signal(barrier, inc=1, device_id=other, device_id_type=MESH)
    pl.semaphore_wait(barrier, 3)

    def gather_copy(step, d):
        rows = half_rows(ring_block(step, d), d)
        return pltpu.make_async_remote_copy(
            src_ref=w_in.at[pl.ds(d * SIDE, SIDE)] if step == 0 else wg.at[rows],
            dst_ref=wg.at[rows],
            send_sem=ag_send.at[d, step],
            recv_sem=ag_recv.at[d, step],
            device_id=up if d == 0 else down,
            device_id_type=MESH,
        )

    def swap(src, dst, i):
        return pltpu.make_async_remote_copy(
            src_ref=src, dst_ref=dst, send_sem=x_send.at[i], recv_sem=x_recv.at[i],
            device_id=partner, device_id_type=MESH,
        )

    gathers = {}

    def gather_step(step):
        for d in range(2):
            if step > 0:
                gathers[step - 1, d].wait_recv()
            if step < NZ - 1:
                gathers[step, d] = gather_copy(step, d)
                gathers[step, d].start()

    sums = {}

    def sum_step(step):
        for part in range(PARTS):
            cols = pl.ds(part * WIDE, WIDE)
            for d in range(2):
                block = ring_block(step + 1, d)
                rows = half_rows(block, d)
                if step == 0:
                    src = grads.at[rows, cols]
                else:
                    sums[step - 1, d, part].wait_recv()
                    slot = ring.at[d, step - 1, :, cols]
                    total = grads[rows, cols].astype(F32) + slot[...].astype(F32)
                    if step == NZ - 1:
                        grad_out[pl.ds(d * SIDE, SIDE), cols] = total
                        continue
                    slot[...] = total.astype(BF16)
                    src = slot
                sums[step, d, part] = pltpu.make_async_remote_copy(
                    src_ref=src,
                    dst_ref=ring.at[d, step, :, cols],
                    send_sem=rs_send.at[d, part, step],
                    recv_sem=rs_recv.at[d, part, step],
                    device_id=up if d == 0 else down,
                    device_id_type=MESH,
                )
                sums[step, d, part].start()

    gather_step(0)
    send_g = swap(g_in, g_far, 0)
    send_g.start()

    load_hid.wait()

    def turn(i, squares):
        tile = hid[:, chunk(i, 256)].astype(F32).T
        ht[chunk(i, 256), :] = tile.astype(BF16)
        return squares + jnp.sum(tile * tile, 0, keepdims=True)

    squares = lax.fori_loop(0, DW // 256, turn, jnp.zeros((1, TOK), F32))
    inverse = 1.0 / jnp.sqrt(squares * (1.0 / DW) + EPSILON)

    def normalise(i, _):
        for d in range(2):
            rows = pl.ds(pl.multiple_of((2 * i + d) * ROWS, 16), ROWS)
            n_halves[d, pl.ds(pl.multiple_of(i * ROWS, 16), ROWS), :] = (
                ht[rows, :].astype(F32) * inverse
            ).astype(BF16)
        return 0

    lax.fori_loop(0, NZ, normalise, 0)
    send_n = swap(n_halves.at[1 - side], n_far, 1)
    send_n.start()

    load_g.wait()
    load_w.wait()
    for step in range(1, 6):
        gather_step(step)

    send_g.wait_recv()
    send_n.wait_recv()

    def gradient_tile(i, _):
        rows = chunk(i, 256)
        a, b = n_halves[side, rows, :], n_far[rows, :]
        for part in range(4):
            cols = pl.ds(part * 512, 512)
            term = dot_nn(a, g_own[:, cols]) + dot_nn(b, g_far[:, cols])
            grads[rows, cols] = (term * SCALE).astype(BF16)
        return 0

    lax.fori_loop(0, HALF // 256, gradient_tile, 0)
    gather_step(6)
    sum_step(0)

    def rows_of(i, _):
        rows = chunk(i, 256)
        n_rows[0, :, rows] = n_halves[side, rows, :].astype(F32).T.astype(BF16)
        n_rows[1, :, rows] = n_far[rows, :].astype(F32).T.astype(BF16)
        return 0

    lax.fori_loop(0, HALF // 256, rows_of, 0)
    gather_step(7)

    def back_tile(far):
        def run(i, _):
            rows = chunk(i, 256)
            if far:
                back_send[rows, :] = (dot_nt(wg[rows, :], g_far[...]) * SCALE).astype(BF16)
            else:
                back_own[rows, :] = dot_nt(wg[rows, :], g_own[...]) * SCALE
            return 0

        lax.fori_loop(0, HALF // 256, run, 0)

    def project_tile(far):
        def run(i, _):
            cols = chunk(i, 512)
            if far:
                p_send[:, cols] = (dot_nn(n_rows[1], wg[:, cols]) * SCALE).astype(BF16)
            else:
                p_own[:, cols] = dot_nn(n_rows[0], wg[:, cols]) * SCALE
            return 0

        lax.fori_loop(0, KVW // 512, run, 0)

    back_tile(True)
    send_back = swap(back_send, back_far, 2)
    send_back.start()
    sum_step(1)
    project_tile(True)
    send_p = swap(p_send, p_far, 3)
    send_p.start()
    sum_step(2)
    back_tile(False)
    sum_step(3)
    project_tile(False)
    sum_step(4)

    send_back.wait_recv()

    def row_pair(i):
        kept = pl.ds(pl.multiple_of(i * ROWS, 16), ROWS)
        own = pl.ds(pl.multiple_of((2 * i + side) * ROWS, 16), ROWS)
        other = pl.ds(pl.multiple_of((2 * i + 1 - side) * ROWS, 16), ROWS)
        return ((back_own[kept, :], own), (back_far[kept, :].astype(F32), other))

    def overlap(i, total):
        for back, rows in row_pair(i):
            total = total + jnp.sum(back * ht[rows, :].astype(F32), 0, keepdims=True)
        return total

    total = lax.fori_loop(0, NZ, overlap, jnp.zeros((1, TOK), F32))
    factor = total * inverse * inverse * (1.0 / DW)

    def back_norm(i, _):
        for back, rows in row_pair(i):
            igt[rows, :] = (back - ht[rows, :].astype(F32) * factor) * inverse
        return 0

    lax.fori_loop(0, NZ, back_norm, 0)

    def turn_back(i, _):
        ig_rows[:, chunk(i, 256)] = igt[chunk(i, 256), :].T.astype(BF16)
        return 0

    lax.fori_loop(0, DW // 256, turn_back, 0)
    store_ig = pltpu.make_async_copy(ig_rows, ig_out, local.at[3])
    store_ig.start()
    sum_step(5)

    send_p.wait_recv()

    def finish(i, _):
        cols = chunk(i, 512)
        p_rows[:, cols] = (p_own[:, cols] + p_far[:, cols].astype(F32)).astype(BF16)
        return 0

    lax.fori_loop(0, KVW // 512, finish, 0)
    store_p = pltpu.make_async_copy(p_rows, proj_out, local.at[4])
    store_p.start()
    sum_step(6)
    sum_step(7)

    store_ig.wait()
    store_p.wait()
    for copy in (send_g, send_n, send_back, send_p):
        copy.wait_send()
    for copy in gathers.values():
        copy.wait_send()
    for copy in sums.values():
        copy.wait_send()


def step_kernel(hidden, weights, cot):
    anywhere = pl.BlockSpec(memory_space=pl.ANY)
    vmem = pltpu.VMEM
    return pl.pallas_call(
        kernel,
        out_shape=(
            jax.ShapeDtypeStruct((TOK, KVW), BF16),
            jax.ShapeDtypeStruct((TOK, DW), BF16),
            jax.ShapeDtypeStruct((ROWS, KVW), F32),
        ),
        in_specs=[anywhere] * 3,
        out_specs=(anywhere, anywhere, pl.BlockSpec(memory_space=pltpu.VMEM)),
        scratch_shapes=[
            vmem((TOK, DW), BF16),
            vmem((TOK, KVW), BF16),
            vmem((TOK, KVW), BF16),
            vmem((DW, TOK), BF16),
            vmem((2, HALF, TOK), BF16),
            vmem((HALF, TOK), BF16),
            vmem((2, TOK, HALF), BF16),
            vmem((HALF, KVW), BF16),
            vmem((HALF, KVW), BF16),
            vmem((2, NZ - 1, SIDE, KVW), BF16),
            vmem((HALF, TOK), F32),
            vmem((HALF, TOK), BF16),
            vmem((HALF, TOK), BF16),
            vmem((TOK, KVW), F32),
            vmem((TOK, KVW), BF16),
            vmem((TOK, KVW), BF16),
            vmem((DW, TOK), F32),
            vmem((TOK, DW), BF16),
            vmem((TOK, KVW), BF16),
            pltpu.SemaphoreType.DMA((2, NZ - 1)),
            pltpu.SemaphoreType.DMA((2, NZ - 1)),
            pltpu.SemaphoreType.DMA((2, PARTS, NZ - 1)),
            pltpu.SemaphoreType.DMA((2, PARTS, NZ - 1)),
            pltpu.SemaphoreType.DMA((4,)),
            pltpu.SemaphoreType.DMA((4,)),
            pltpu.SemaphoreType.DMA((5,)),
        ],
        compiler_params=pltpu.CompilerParams(
            collective_id=0, has_side_effects=True, vmem_limit_bytes=56 << 20
        ),
        cost_estimate=pl.CostEstimate(
            flops=6 * TOK * DW * KVW, bytes_accessed=600 << 20, transcendentals=0
        ),
    )(hidden, weights, cot)


def body(hidden_in, local_weights, cotangent, global_weights, outer_momentum, step_index):
    frag_cols = KVW // FRAGS
    start = step_index[0] % FRAGS * frag_cols
    local_frag = lax.dynamic_slice_in_dim(local_weights[0], start, frag_cols, 1)
    replicas = lax.axis_size("replica")
    total = lax.psum(local_frag, "replica").astype(F32)
    projected, input_grad, gradient = step_kernel(hidden_in[0], local_weights[0], cotangent[0])
    global_frag = lax.dynamic_slice_in_dim(global_weights, start, frag_cols, 1)
    moment_frag = lax.dynamic_slice_in_dim(outer_momentum, start, frag_cols, 1)
    new_global, new_momentum = outer_update(global_frag, moment_frag, total / replicas)
    updated = local_weights[0].astype(F32) - INNER_RATE * gradient
    upd_frag = lax.dynamic_slice_in_dim(updated, start, frag_cols, 1)
    mixed = MIX_KEEP * upd_frag + (1.0 - MIX_KEEP) * new_global
    new_weights = lax.dynamic_update_slice_in_dim(updated, mixed, start, 1).astype(BF16)
    return (projected[None], input_grad[None], new_weights[None], new_global, new_momentum)


def solution(mesh):
    placed = (
        P("replica", "fsdp", None),
        P("replica", "fsdp", None),
        P("replica", "fsdp", None),
        P("fsdp", None),
        P("fsdp", None),
        P(),
    )
    return jax.shard_map(
        body,
        mesh=mesh,
        in_specs=placed,
        out_specs=(
            P("replica", "fsdp", None),
            P("replica", "fsdp", None),
            P("replica", "fsdp", None),
            P("fsdp", None),
            P("fsdp", None),
        ),
        check_vma=False,
    )
```

```python
import functools
import math

import jax
import jax.numpy as jnp
from jax import lax
from jax.experimental import pallas as pl
from jax.experimental.pallas import tpu as pltpu
from jax.sharding import PartitionSpec as P

KVW = 2048
FRAGS = 4
FRAGW = KVW // FRAGS
REPLICAS = 16
DW = 3584
HALF = DW // 2
TOK = 256
ROWS = 224
SIDE = ROWS // 2
NZ = 8
PARTS = 2
WIDE = KVW // PARTS
SCALE = 1.0 / math.sqrt(DW)

EPSILON = 1e-05
INNER_RATE = 0.25
OUTER_RATE = 0.7
NESTEROV = 0.9
MIX_KEEP = 0.5

MESH = pl.DeviceIdType.MESH
F32 = jnp.float32
BF16 = jnp.bfloat16


def outer_update(global_part, moment_part, mean_part):
    delta = global_part - mean_part
    moment_next = NESTEROV * moment_part + delta
    global_next = global_part - OUTER_RATE * (delta + NESTEROV * moment_next)
    return (global_next, moment_next)


def dot_nn(a, b):
    return jnp.dot(a, b, preferred_element_type=F32)


def dot_nt(a, b):
    return lax.dot_general(a, b, (((1,), (1,)), ((), ())), preferred_element_type=F32)


def chunk(i, size):
    return pl.ds(pl.multiple_of(i * size, size), size)


def kernel(
    step_in, hid_in, w_in, g_in, global_in, moment_in,
    proj_out, ig_out, weights_out, global_out, moment_out,
    hid, g_own, g_far, ht, n_halves, n_far, n_rows, wg, grads, ring,
    back_own, back_send, back_far, p_own, p_send, p_far, p_rows,
    old_global, old_moment, frags, global_next, moment_next, new_rows,
    ag_send, ag_recv, rs_send, rs_recv, x_send, x_recv, f_send, f_recv, local,
):
    replica = lax.axis_index("replica")
    place = lax.axis_index("fsdp")
    z, side = place // 2, lax.rem(place, 2)
    up = (replica, lax.rem(z + 1, NZ) * 2 + side)
    down = (replica, lax.rem(z + NZ - 1, NZ) * 2 + side)
    partner = (replica, z * 2 + 1 - side)
    quad = lax.rem(replica, 4)
    core_twin = (replica + 1 - 2 * lax.rem(replica, 2), place)
    lane_twin = (replica - quad + lax.rem(quad + 2, 4), place)
    columns = [(lax.rem(replica + 4 * k, 16), place) for k in range(1, 4)]
    turn_now = lax.rem(step_in[0], FRAGS).astype(F32)
    chosen = [1.0 - jnp.minimum(jnp.abs(turn_now - f), 1.0) for f in range(FRAGS)]
    own_rows = pl.ds(pl.multiple_of(z * ROWS, 16), ROWS)

    def half_rows(block, d):
        return pl.ds(pl.multiple_of(block * ROWS + d * SIDE, 16), SIDE)

    def ring_block(step, d):
        return lax.rem(z - step + 2 * NZ, NZ) if d == 0 else lax.rem(z + step, NZ)

    load_hid = pltpu.make_async_copy(hid_in, hid, local.at[0])
    load_g = pltpu.make_async_copy(g_in, g_own, local.at[1])
    load_w = pltpu.make_async_copy(w_in, wg.at[own_rows], local.at[2])
    load_global = pltpu.make_async_copy(global_in, old_global, local.at[3])
    load_moment = pltpu.make_async_copy(moment_in, old_moment, local.at[4])

    barrier = pltpu.get_barrier_semaphore()
    others = (up, down, partner, core_twin, lane_twin, *columns)
    for other in others:
        pl.semaphore_signal(barrier, inc=1, device_id=other, device_id_type=MESH)
    load_hid.start()
    load_w.start()
    load_g.start()
    load_global.start()
    load_moment.start()
    pl.semaphore_wait(barrier, len(others))

    def gather_copy(step, d):
        rows = half_rows(ring_block(step, d), d)
        return pltpu.make_async_remote_copy(
            src_ref=w_in.at[pl.ds(d * SIDE, SIDE)] if step == 0 else wg.at[rows],
            dst_ref=wg.at[rows],
            send_sem=ag_send.at[d, step],
            recv_sem=ag_recv.at[d, step],
            device_id=up if d == 0 else down,
            device_id_type=MESH,
        )

    def swap(src, dst, i):
        return pltpu.make_async_remote_copy(
            src_ref=src, dst_ref=dst, send_sem=x_send.at[i], recv_sem=x_recv.at[i],
            device_id=partner, device_id_type=MESH,
        )

    def frag_copy(src, dst, i, other):
        return pltpu.make_async_remote_copy(
            src_ref=frags.at[src], dst_ref=frags.at[dst],
            send_sem=f_send.at[i], recv_sem=f_recv.at[i],
            device_id=other, device_id_type=MESH,
        )

    gathers = {}

    def gather_step(step):
        for d in range(2):
            if step > 0:
                gathers[step - 1, d].wait_recv()
            if step < NZ - 1:
                gathers[step, d] = gather_copy(step, d)
                gathers[step, d].start()

    stores = []

    def store(src, dst, i):
        copy = pltpu.make_async_copy(src, dst, local.at[i])
        copy.start()
        stores.append(copy)

    def new_weights(d, part, rows, total):
        kept = pl.ds(d * SIDE, SIDE)
        blend = global_next[kept, :]
        for f in range(part * FRAGS // PARTS, (part + 1) * FRAGS // PARTS):
            cols = pl.ds(f * FRAGW, FRAGW)
            first = f * FRAGW - part * WIDE
            updated = wg[rows, cols].astype(F32) - INNER_RATE * total[:, first : first + FRAGW]
            keep = 1.0 - (1.0 - MIX_KEEP) * chosen[f]
            new_rows[kept, cols] = (updated * keep + blend * (1.0 - keep)).astype(BF16)
        cols = pl.ds(part * WIDE, WIDE)
        store(new_rows.at[kept, cols], weights_out.at[kept, cols], 9 + part * 2 + d)

    sums = {}

    def sum_step(step):
        for part in range(PARTS):
            cols = pl.ds(part * WIDE, WIDE)
            for d in range(2):
                block = ring_block(step + 1, d)
                rows = half_rows(block, d)
                if step == 0:
                    src = grads.at[rows, cols]
                else:
                    sums[step - 1, d, part].wait_recv()
                    slot = ring.at[d, step - 1, :, cols]
                    total = grads[rows, cols].astype(F32) + slot[...].astype(F32)
                    if step == NZ - 1:
                        new_weights(d, part, rows, total)
                        continue
                    slot[...] = total.astype(BF16)
                    src = slot
                sums[step, d, part] = pltpu.make_async_remote_copy(
                    src_ref=src,
                    dst_ref=ring.at[d, step, :, cols],
                    send_sem=rs_send.at[d, part, step],
                    recv_sem=rs_recv.at[d, part, step],
                    device_id=up if d == 0 else down,
                    device_id_type=MESH,
                )
                sums[step, d, part].start()

    gather_step(0)
    send_g = swap(g_in, g_far, 0)
    send_g.start()

    load_hid.wait()

    def turn(i, squares):
        tile = hid[:, chunk(i, 256)].astype(F32).T
        ht[chunk(i, 256), :] = tile.astype(BF16)
        return squares + jnp.sum(tile * tile, 0, keepdims=True)

    squares = lax.fori_loop(0, DW // 256, turn, jnp.zeros((1, TOK), F32))
    inverse = 1.0 / jnp.sqrt(squares * (1.0 / DW) + EPSILON)

    def normalise(i, _):
        for d in range(2):
            rows = pl.ds(pl.multiple_of((2 * i + d) * ROWS, 16), ROWS)
            n_halves[d, pl.ds(pl.multiple_of(i * ROWS, 16), ROWS), :] = (
                ht[rows, :].astype(F32) * inverse
            ).astype(BF16)
        return 0

    lax.fori_loop(0, NZ, normalise, 0)
    send_n = swap(n_halves.at[1 - side], n_far, 1)
    send_n.start()

    def fragment(ref, rows):
        return sum(
            ref[rows, pl.ds(f * FRAGW, FRAGW)].astype(F32) * chosen[f] for f in range(FRAGS)
        )

    load_w.wait()
    frags[0] = fragment(wg, own_rows).astype(BF16)
    sent_frags = [frag_copy(0, 1, 0, core_twin)]
    sent_frags[0].start()

    load_g.wait()
    gather_step(1)

    gather_step(2)

    sent_frags[0].wait_recv()
    frags[2] = (frags[0].astype(F32) + frags[1].astype(F32)).astype(BF16)
    sent_frags.append(frag_copy(2, 3, 1, lane_twin))
    sent_frags[1].start()
    for step in range(3, 6):
        gather_step(step)

    send_g.wait_recv()
    send_n.wait_recv()

    def gradient_tile(i, _):
        rows = chunk(i, 256)
        a, b = n_halves[side, rows, :], n_far[rows, :]
        for part in range(4):
            cols = pl.ds(part * 512, 512)
            term = dot_nn(a, g_own[:, cols]) + dot_nn(b, g_far[:, cols])
            grads[rows, cols] = (term * SCALE).astype(BF16)
        return 0

    lax.fori_loop(0, HALF // 256, gradient_tile, 0)
    gather_step(6)
    sum_step(0)

    def rows_of(i, _):
        rows = chunk(i, 256)
        n_rows[0, :, rows] = n_halves[side, rows, :].astype(F32).T.astype(BF16)
        n_rows[1, :, rows] = n_far[rows, :].astype(F32).T.astype(BF16)
        return 0

    lax.fori_loop(0, HALF // 256, rows_of, 0)
    gather_step(7)

    sent_frags[1].wait_recv()
    frags[4] = (frags[2].astype(F32) + frags[3].astype(F32)).astype(BF16)
    for k in range(3):
        sent_frags.append(frag_copy(4, 5 + k, 2 + k, columns[k]))
        sent_frags[2 + k].start()

    def back_tile(far):
        def run(i, _):
            rows = chunk(i, 256)
            if far:
                back_send[rows, :] = (dot_nt(wg[rows, :], g_far[...]) * SCALE).astype(BF16)
            else:
                back_own[rows, :] = dot_nt(wg[rows, :], g_own[...]) * SCALE
            return 0

        lax.fori_loop(0, HALF // 256, run, 0)

    def project_tile(far):
        def run(i, _):
            cols = chunk(i, 512)
            if far:
                p_send[:, cols] = (dot_nn(n_rows[1], wg[:, cols]) * SCALE).astype(BF16)
            else:
                p_own[:, cols] = dot_nn(n_rows[0], wg[:, cols]) * SCALE
            return 0

        lax.fori_loop(0, KVW // 512, run, 0)

    back_tile(True)
    send_back = swap(back_send, back_far, 2)
    send_back.start()
    sum_step(1)
    project_tile(True)
    send_p = swap(p_send, p_far, 3)
    send_p.start()
    sum_step(2)
    back_tile(False)
    sum_step(3)

    load_global.wait()
    load_moment.wait()
    for k in range(3):
        sent_frags[2 + k].wait_recv()
    mean = frags[4].astype(F32)
    for k in range(3):
        mean = mean + frags[5 + k].astype(F32)
    every = pl.ds(0, ROWS)
    global_next[...], moment_next[...] = outer_update(
        fragment(old_global, every), fragment(old_moment, every), mean * (1.0 / REPLICAS)
    )
    store(global_next, global_out, 5)
    store(moment_next, moment_out, 6)
    project_tile(False)
    sum_step(4)

    send_back.wait_recv()

    def row_pair(i):
        kept = pl.ds(pl.multiple_of(i * ROWS, 16), ROWS)
        own = pl.ds(pl.multiple_of((2 * i + side) * ROWS, 16), ROWS)
        other = pl.ds(pl.multiple_of((2 * i + 1 - side) * ROWS, 16), ROWS)
        return ((back_own[kept, :], own), (back_far[kept, :].astype(F32), other))

    def overlap(i, total):
        for back, rows in row_pair(i):
            total = total + jnp.sum(back * ht[rows, :].astype(F32), 0, keepdims=True)
        return total

    total = lax.fori_loop(0, NZ, overlap, jnp.zeros((1, TOK), F32))
    factor = total * inverse * inverse * (1.0 / DW)

    def back_norm(i, _):
        for back, rows in row_pair(i):
            ht[rows, :] = ((back - ht[rows, :].astype(F32) * factor) * inverse).astype(BF16)
        return 0

    lax.fori_loop(0, NZ, back_norm, 0)

    def turn_back(i, _):
        hid[:, chunk(i, 256)] = ht[chunk(i, 256), :].astype(F32).T.astype(BF16)
        return 0

    lax.fori_loop(0, DW // 256, turn_back, 0)
    store(hid, ig_out, 7)
    sum_step(5)

    send_p.wait_recv()

    def finish(i, _):
        cols = chunk(i, 512)
        p_rows[:, cols] = (p_own[:, cols] + p_far[:, cols].astype(F32)).astype(BF16)
        return 0

    lax.fori_loop(0, KVW // 512, finish, 0)
    store(p_rows, proj_out, 8)
    sum_step(6)
    sum_step(7)

    for copy in stores:
        copy.wait()
    for copy in (send_g, send_n, send_back, send_p, *sent_frags):
        copy.wait_send()
    for copy in gathers.values():
        copy.wait_send()
    for copy in sums.values():
        copy.wait_send()


def copy_kernel(*refs):
    count = len(refs) // 2
    copies = [
        pltpu.make_async_copy(refs[i], refs[count + i], refs[-1].at[i]) for i in range(count)
    ]
    for copy in copies:
        copy.start()
    for copy in copies:
        copy.wait()


def copy_out(arrays):
    anywhere = pl.BlockSpec(memory_space=pl.ANY)
    return pl.pallas_call(
        copy_kernel,
        out_shape=tuple(jax.ShapeDtypeStruct(a.shape, a.dtype) for a in arrays),
        in_specs=[pl.BlockSpec(memory_space=pltpu.VMEM)] * len(arrays),
        out_specs=(anywhere,) * len(arrays),
        scratch_shapes=[pltpu.SemaphoreType.DMA((len(arrays),))],
    )(*arrays)


def step_kernel(step, hidden, weights, cot, global_weights, moment):
    anywhere = pl.BlockSpec(memory_space=pl.ANY)
    vmem = pltpu.VMEM
    return pl.pallas_call(
        kernel,
        out_shape=(
            jax.ShapeDtypeStruct((TOK, KVW), BF16),
            jax.ShapeDtypeStruct((TOK, DW), BF16),
            jax.ShapeDtypeStruct((ROWS, KVW), BF16),
            jax.ShapeDtypeStruct((ROWS, FRAGW), F32),
            jax.ShapeDtypeStruct((ROWS, FRAGW), F32),
        ),
        in_specs=[pl.BlockSpec(memory_space=pltpu.SMEM)] + [anywhere] * 5,
        out_specs=(anywhere,) * 5,
        scratch_shapes=[
            vmem((TOK, DW), BF16),
            vmem((TOK, KVW), BF16),
            vmem((TOK, KVW), BF16),
            vmem((DW, TOK), BF16),
            vmem((2, HALF, TOK), BF16),
            vmem((HALF, TOK), BF16),
            vmem((2, TOK, HALF), BF16),
            vmem((HALF, KVW), BF16),
            vmem((HALF, KVW), BF16),
            vmem((2, NZ - 1, SIDE, KVW), BF16),
            vmem((HALF, TOK), F32),
            vmem((HALF, TOK), BF16),
            vmem((HALF, TOK), BF16),
            vmem((TOK, KVW), F32),
            vmem((TOK, KVW), BF16),
            vmem((TOK, KVW), BF16),
            vmem((TOK, KVW), BF16),
            vmem((ROWS, KVW), F32),
            vmem((ROWS, KVW), F32),
            vmem((8, ROWS, FRAGW), BF16),
            vmem((ROWS, FRAGW), F32),
            vmem((ROWS, FRAGW), F32),
            vmem((ROWS, KVW), BF16),
            pltpu.SemaphoreType.DMA((2, NZ - 1)),
            pltpu.SemaphoreType.DMA((2, NZ - 1)),
            pltpu.SemaphoreType.DMA((2, PARTS, NZ - 1)),
            pltpu.SemaphoreType.DMA((2, PARTS, NZ - 1)),
            pltpu.SemaphoreType.DMA((4,)),
            pltpu.SemaphoreType.DMA((4,)),
            pltpu.SemaphoreType.DMA((5,)),
            pltpu.SemaphoreType.DMA((5,)),
            pltpu.SemaphoreType.DMA((9 + 2 * PARTS,)),
        ],
        compiler_params=pltpu.CompilerParams(
            collective_id=0, has_side_effects=True, vmem_limit_bytes=56 << 20
        ),
        cost_estimate=pl.CostEstimate(
            flops=6 * TOK * DW * KVW, bytes_accessed=600 << 20, transcendentals=0
        ),
    )(step, hidden, weights, cot, global_weights, moment)


def body(hidden_in, local_weights, cotangent, global_weights, outer_momentum, step_index):
    results = step_kernel(
        step_index, hidden_in[0], local_weights[0], cotangent[0], global_weights, outer_momentum
    )
    projected, input_grad, new_weights, new_global, new_momentum = copy_out(results)
    return (projected[None], input_grad[None], new_weights[None], new_global, new_momentum)


def solution(mesh):
    placed = (
        P("replica", "fsdp", None),
        P("replica", "fsdp", None),
        P("replica", "fsdp", None),
        P("fsdp", None),
        P("fsdp", None),
        P(),
    )
    return jax.shard_map(
        body,
        mesh=mesh,
        in_specs=placed,
        out_specs=(
            P("replica", "fsdp", None),
            P("replica", "fsdp", None),
            P("replica", "fsdp", None),
            P("fsdp", None),
            P("fsdp", None),
        ),
        check_vma=False,
    )
```

```python
import functools
import math

import jax
import jax.numpy as jnp
from jax import lax
from jax.experimental import pallas as pl
from jax.experimental.pallas import tpu as pltpu
from jax.sharding import PartitionSpec as P

KVW = 2048
FRAGS = 4
FRAGW = KVW // FRAGS
REPLICAS = 16
DW = 3584
HALF = DW // 2
TOK = 256
ROWS = 224
SIDE = ROWS // 2
NZ = 8
PARTS = 2
WIDE = KVW // PARTS
SCALE = 1.0 / math.sqrt(DW)

EPSILON = 1e-05
INNER_RATE = 0.25
OUTER_RATE = 0.7
NESTEROV = 0.9
MIX_KEEP = 0.5

MESH = pl.DeviceIdType.MESH
F32 = jnp.float32
BF16 = jnp.bfloat16


def outer_update(global_part, moment_part, mean_part):
    delta = global_part - mean_part
    moment_next = NESTEROV * moment_part + delta
    global_next = global_part - OUTER_RATE * (delta + NESTEROV * moment_next)
    return (global_next, moment_next)


def dot_nn(a, b):
    return jnp.dot(a, b, preferred_element_type=F32)


def dot_nt(a, b):
    return lax.dot_general(a, b, (((1,), (1,)), ((), ())), preferred_element_type=F32)


def chunk(i, size):
    return pl.ds(pl.multiple_of(i * size, size), size)


def kernel(
    step_in, hid_in, w_in, g_in, global_in, moment_in,
    proj_out, ig_out, weights_out, global_out, moment_out,
    hid, g_own, g_far, ht, n_halves, n_far, n_rows, wg, grads, ring,
    step, back_own, back_send, back_far, p_own, p_send, p_far,
    old_global, old_moment, frags,
    ag_send, ag_recv, rs_send, rs_recv, x_send, x_recv, f_send, f_recv, local,
):
    replica = lax.axis_index("replica")
    place = lax.axis_index("fsdp")
    z, side = place // 2, lax.rem(place, 2)
    up = (replica, lax.rem(z + 1, NZ) * 2 + side)
    down = (replica, lax.rem(z + NZ - 1, NZ) * 2 + side)
    partner = (replica, z * 2 + 1 - side)
    quad = lax.rem(replica, 4)
    core_twin = (replica + 1 - 2 * lax.rem(replica, 2), place)
    lane_twin = (replica - quad + lax.rem(quad + 2, 4), place)
    columns = [(lax.rem(replica + 4 * k, 16), place) for k in range(1, 4)]
    own_rows = pl.ds(pl.multiple_of(z * ROWS, 16), ROWS)

    def half_rows(block, d):
        return pl.ds(pl.multiple_of(block * ROWS + d * SIDE, 16), SIDE)

    def ring_block(step, d):
        return lax.rem(z - step + 2 * NZ, NZ) if d == 0 else lax.rem(z + step, NZ)

    load_step = pltpu.make_async_copy(step_in, step, local.at[5])
    load_step.start()
    load_hid = pltpu.make_async_copy(hid_in, hid, local.at[0])
    load_g = pltpu.make_async_copy(g_in, g_own, local.at[1])
    load_w = pltpu.make_async_copy(w_in, wg.at[own_rows], local.at[2])
    load_global = pltpu.make_async_copy(global_in, old_global, local.at[3])
    load_moment = pltpu.make_async_copy(moment_in, old_moment, local.at[4])

    barrier = pltpu.get_barrier_semaphore()
    others = (up, down, partner, core_twin, lane_twin, *columns)
    for other in others:
        pl.semaphore_signal(barrier, inc=1, device_id=other, device_id_type=MESH)
    load_hid.start()
    load_w.start()
    load_g.start()
    load_global.start()
    load_moment.start()
    pl.semaphore_wait(barrier, len(others))

    def gather_copy(step, d, part):
        rows, cols = half_rows(ring_block(step, d), d), pl.ds(part * WIDE, WIDE)
        return pltpu.make_async_remote_copy(
            src_ref=w_in.at[pl.ds(d * SIDE, SIDE), cols] if step == 0 else wg.at[rows, cols],
            dst_ref=wg.at[rows, cols],
            send_sem=ag_send.at[d, part, step],
            recv_sem=ag_recv.at[d, part, step],
            device_id=up if d == 0 else down,
            device_id_type=MESH,
        )

    def swap(src, dst, i):
        return pltpu.make_async_remote_copy(
            src_ref=src, dst_ref=dst, send_sem=x_send.at[i], recv_sem=x_recv.at[i],
            device_id=partner, device_id_type=MESH,
        )

    def frag_copy(src, dst, i, other):
        return pltpu.make_async_remote_copy(
            src_ref=frags.at[src], dst_ref=frags.at[dst],
            send_sem=f_send.at[i], recv_sem=f_recv.at[i],
            device_id=other, device_id_type=MESH,
        )

    gathers = {}

    def gather_step(step):
        for part in range(PARTS):
            for d in range(2):
                if step > 0:
                    gathers[step - 1, d, part].wait_recv()
                if step < NZ - 1:
                    gathers[step, d, part] = gather_copy(step, d, part)
                    gathers[step, d, part].start()

    def new_weights(d, part, rows, total):
        kept = pl.ds(d * SIDE, SIDE)
        blend = global_out[kept, :]
        for f in range(part * FRAGS // PARTS, (part + 1) * FRAGS // PARTS):
            cols = pl.ds(f * FRAGW, FRAGW)
            first = f * FRAGW - part * WIDE
            updated = wg[rows, cols].astype(F32) - INNER_RATE * total[:, first : first + FRAGW]
            keep = 1.0 - (1.0 - MIX_KEEP) * chosen[f]
            weights_out[kept, cols] = (updated * keep + blend * (1.0 - keep)).astype(BF16)

    sums = {}

    def sum_step(step):
        for part in range(PARTS):
            cols = pl.ds(part * WIDE, WIDE)
            for d in range(2):
                block = ring_block(step + 1, d)
                rows = half_rows(block, d)
                if step == 0:
                    src = grads.at[rows, cols]
                else:
                    sums[step - 1, d, part].wait_recv()
                    slot = ring.at[d, step - 1, :, cols]
                    total = grads[rows, cols].astype(F32) + slot[...].astype(F32)
                    if step == NZ - 1:
                        new_weights(d, part, rows, total)
                        continue
                    slot[...] = total.astype(BF16)
                    src = slot
                sums[step, d, part] = pltpu.make_async_remote_copy(
                    src_ref=src,
                    dst_ref=ring.at[d, step, :, cols],
                    send_sem=rs_send.at[d, part, step],
                    recv_sem=rs_recv.at[d, part, step],
                    device_id=up if d == 0 else down,
                    device_id_type=MESH,
                )
                sums[step, d, part].start()

    gather_step(0)
    send_g = swap(g_in, g_far, 0)
    send_g.start()

    load_hid.wait()

    def turn(i, squares):
        tile = hid[:, chunk(i, 256)].astype(F32).T
        ht[chunk(i, 256), :] = tile.astype(BF16)
        return squares + jnp.sum(tile * tile, 0, keepdims=True)

    squares = lax.fori_loop(0, DW // 256, turn, jnp.zeros((1, TOK), F32))
    inverse = 1.0 / jnp.sqrt(squares * (1.0 / DW) + EPSILON)

    def normalise(i, _):
        for d in range(2):
            rows = pl.ds(pl.multiple_of((2 * i + d) * ROWS, 16), ROWS)
            n_halves[d, pl.ds(pl.multiple_of(i * ROWS, 16), ROWS), :] = (
                ht[rows, :].astype(F32) * inverse
            ).astype(BF16)
        return 0

    lax.fori_loop(0, NZ, normalise, 0)
    send_n = swap(n_halves.at[1 - side], n_far, 1)
    send_n.start()

    load_step.wait()
    turn_now = lax.rem(step[0], FRAGS).astype(F32)
    chosen = [1.0 - jnp.minimum(jnp.abs(turn_now - f), 1.0) for f in range(FRAGS)]

    def fragment(ref, rows):
        return sum(
            ref[rows, pl.ds(f * FRAGW, FRAGW)].astype(F32) * chosen[f] for f in range(FRAGS)
        )

    load_w.wait()
    frags[0] = fragment(wg, own_rows).astype(BF16)
    sent_frags = [frag_copy(0, 1, 0, core_twin)]
    sent_frags[0].start()

    load_g.wait()
    gather_step(1)

    gather_step(2)

    sent_frags[0].wait_recv()
    frags[2] = (frags[0].astype(F32) + frags[1].astype(F32)).astype(BF16)
    sent_frags.append(frag_copy(2, 3, 1, lane_twin))
    sent_frags[1].start()
    for step in range(3, 6):
        gather_step(step)

    send_g.wait_recv()
    send_n.wait_recv()

    def gradient_tile(i, _):
        rows = chunk(i, 256)
        a, b = n_halves[side, rows, :], n_far[rows, :]
        for part in range(4):
            cols = pl.ds(part * 512, 512)
            term = dot_nn(a, g_own[:, cols]) + dot_nn(b, g_far[:, cols])
            grads[rows, cols] = (term * SCALE).astype(BF16)
        return 0

    lax.fori_loop(0, HALF // 256, gradient_tile, 0)
    gather_step(6)
    sum_step(0)

    def rows_of(i, _):
        rows = chunk(i, 256)
        n_rows[0, :, rows] = n_halves[side, rows, :].astype(F32).T.astype(BF16)
        n_rows[1, :, rows] = n_far[rows, :].astype(F32).T.astype(BF16)
        return 0

    lax.fori_loop(0, HALF // 256, rows_of, 0)
    gather_step(7)

    sent_frags[1].wait_recv()
    frags[4] = (frags[2].astype(F32) + frags[3].astype(F32)).astype(BF16)
    for k in range(3):
        sent_frags.append(frag_copy(4, 5 + k, 2 + k, columns[k]))
        sent_frags[2 + k].start()

    def back_tile(far):
        def run(i, _):
            rows = chunk(i, 256)
            if far:
                back_send[rows, :] = (dot_nt(wg[rows, :], g_far[...]) * SCALE).astype(BF16)
            else:
                back_own[rows, :] = dot_nt(wg[rows, :], g_own[...]) * SCALE
            return 0

        lax.fori_loop(0, HALF // 256, run, 0)

    def project_tile(far):
        def run(i, _):
            cols = chunk(i, 512)
            if far:
                p_send[:, cols] = (dot_nn(n_rows[1], wg[:, cols]) * SCALE).astype(BF16)
            else:
                p_own[:, cols] = dot_nn(n_rows[0], wg[:, cols]) * SCALE
            return 0

        lax.fori_loop(0, KVW // 512, run, 0)

    back_tile(True)
    send_back = swap(back_send, back_far, 2)
    send_back.start()
    sum_step(1)
    project_tile(True)
    send_p = swap(p_send, p_far, 3)
    send_p.start()
    sum_step(2)
    back_tile(False)
    sum_step(3)

    load_global.wait()
    load_moment.wait()
    for k in range(3):
        sent_frags[2 + k].wait_recv()
    mean = frags[4].astype(F32)
    for k in range(3):
        mean = mean + frags[5 + k].astype(F32)
    every = pl.ds(0, ROWS)
    global_out[...], moment_out[...] = outer_update(
        fragment(old_global, every), fragment(old_moment, every), mean * (1.0 / REPLICAS)
    )
    project_tile(False)
    sum_step(4)

    send_back.wait_recv()

    def row_pair(i):
        kept = pl.ds(pl.multiple_of(i * ROWS, 16), ROWS)
        own = pl.ds(pl.multiple_of((2 * i + side) * ROWS, 16), ROWS)
        other = pl.ds(pl.multiple_of((2 * i + 1 - side) * ROWS, 16), ROWS)
        return ((back_own[kept, :], own), (back_far[kept, :].astype(F32), other))

    def overlap(i, total):
        for back, rows in row_pair(i):
            total = total + jnp.sum(back * ht[rows, :].astype(F32), 0, keepdims=True)
        return total

    total = lax.fori_loop(0, NZ, overlap, jnp.zeros((1, TOK), F32))
    factor = total * inverse * inverse * (1.0 / DW)

    def back_norm(i, _):
        for back, rows in row_pair(i):
            ht[rows, :] = ((back - ht[rows, :].astype(F32) * factor) * inverse).astype(BF16)
        return 0

    lax.fori_loop(0, NZ, back_norm, 0)

    def turn_back(i, _):
        ig_out[:, chunk(i, 256)] = ht[chunk(i, 256), :].astype(F32).T.astype(BF16)
        return 0

    lax.fori_loop(0, DW // 256, turn_back, 0)
    sum_step(5)

    send_p.wait_recv()

    def finish(i, _):
        cols = chunk(i, 512)
        proj_out[:, cols] = (p_own[:, cols] + p_far[:, cols].astype(F32)).astype(BF16)
        return 0

    lax.fori_loop(0, KVW // 512, finish, 0)
    sum_step(6)
    sum_step(7)

    for copy in (send_g, send_n, send_back, send_p, *sent_frags):
        copy.wait_send()
    for copy in gathers.values():
        copy.wait_send()
    for copy in sums.values():
        copy.wait_send()


def copy_kernel(*refs):
    count = len(refs) // 2
    copies = [
        pltpu.make_async_copy(refs[i], refs[count + i], refs[-1].at[i]) for i in range(count)
    ]
    for copy in copies:
        copy.start()
    for copy in copies:
        copy.wait()


def copy_out(arrays):
    anywhere = pl.BlockSpec(memory_space=pl.ANY)
    return pl.pallas_call(
        copy_kernel,
        out_shape=tuple(jax.ShapeDtypeStruct(a.shape, a.dtype) for a in arrays),
        in_specs=[pl.BlockSpec(memory_space=pltpu.VMEM)] * len(arrays),
        out_specs=(anywhere,) * len(arrays),
        scratch_shapes=[pltpu.SemaphoreType.DMA((len(arrays),))],
        compiler_params=pltpu.CompilerParams(vmem_limit_bytes=2 << 20),
    )(*arrays)


def step_kernel(step, hidden, weights, cot, global_weights, moment):
    anywhere = pl.BlockSpec(memory_space=pl.ANY)
    vmem = pltpu.VMEM
    return pl.pallas_call(
        kernel,
        out_shape=(
            vmem((TOK, KVW), BF16),
            vmem((TOK, DW), BF16),
            vmem((ROWS, KVW), BF16),
            vmem((ROWS, FRAGW), F32),
            vmem((ROWS, FRAGW), F32),
        ),
        in_specs=[pl.BlockSpec(memory_space=pltpu.HBM)] + [anywhere] * 5,
        out_specs=(pl.BlockSpec(memory_space=pltpu.VMEM),) * 5,
        scratch_shapes=[
            vmem((TOK, DW), BF16),
            vmem((TOK, KVW), BF16),
            vmem((TOK, KVW), BF16),
            vmem((DW, TOK), BF16),
            vmem((2, HALF, TOK), BF16),
            vmem((HALF, TOK), BF16),
            vmem((2, TOK, HALF), BF16),
            vmem((HALF, KVW), BF16),
            vmem((HALF, KVW), BF16),
            vmem((2, NZ - 1, SIDE, KVW), BF16),
            pltpu.SMEM((1,), jnp.int32),
            vmem((HALF, TOK), F32),
            vmem((HALF, TOK), BF16),
            vmem((HALF, TOK), BF16),
            vmem((TOK, KVW), F32),
            vmem((TOK, KVW), BF16),
            vmem((TOK, KVW), BF16),
            vmem((ROWS, KVW), F32),
            vmem((ROWS, KVW), F32),
            vmem((8, ROWS, FRAGW), BF16),
            pltpu.SemaphoreType.DMA((2, PARTS, NZ - 1)),
            pltpu.SemaphoreType.DMA((2, PARTS, NZ - 1)),
            pltpu.SemaphoreType.DMA((2, PARTS, NZ - 1)),
            pltpu.SemaphoreType.DMA((2, PARTS, NZ - 1)),
            pltpu.SemaphoreType.DMA((4,)),
            pltpu.SemaphoreType.DMA((4,)),
            pltpu.SemaphoreType.DMA((5,)),
            pltpu.SemaphoreType.DMA((5,)),
            pltpu.SemaphoreType.DMA((6,)),
        ],
        compiler_params=pltpu.CompilerParams(
            collective_id=0, has_side_effects=True, vmem_limit_bytes=54 << 20
        ),
        cost_estimate=pl.CostEstimate(
            flops=6 * TOK * DW * KVW, bytes_accessed=600 << 20, transcendentals=0
        ),
    )(step, hidden, weights, cot, global_weights, moment)


def body(hidden_in, local_weights, cotangent, global_weights, outer_momentum, step_index):
    results = step_kernel(
        step_index, hidden_in[0], local_weights[0], cotangent[0], global_weights, outer_momentum
    )
    projected, input_grad, new_weights, new_global, new_momentum = copy_out(results)
    return (projected[None], input_grad[None], new_weights[None], new_global, new_momentum)


def solution(mesh):
    placed = (
        P("replica", "fsdp", None),
        P("replica", "fsdp", None),
        P("replica", "fsdp", None),
        P("fsdp", None),
        P("fsdp", None),
        P(),
    )
    return jax.shard_map(
        body,
        mesh=mesh,
        in_specs=placed,
        out_specs=(
            P("replica", "fsdp", None),
            P("replica", "fsdp", None),
            P("replica", "fsdp", None),
            P("fsdp", None),
            P("fsdp", None),
        ),
        check_vma=False,
    )
```

```python
import functools
import math

import jax
import jax.numpy as jnp
from jax import lax
from jax.experimental import pallas as pl
from jax.experimental.pallas import tpu as pltpu
from jax.sharding import PartitionSpec as P

KVW = 2048
FRAGS = 4
FRAGW = KVW // FRAGS
REPLICAS = 16
DW = 3584
HALF = DW // 2
TOK = 256
ROWS = 224
SIDE = ROWS // 2
NZ = 8
PARTS = 2
WIDE = KVW // PARTS
SCALE = 1.0 / math.sqrt(DW)

EPSILON = 1e-05
INNER_RATE = 0.25
OUTER_RATE = 0.7
NESTEROV = 0.9
MIX_KEEP = 0.5

MESH = pl.DeviceIdType.MESH
F32 = jnp.float32
BF16 = jnp.bfloat16


def outer_update(global_part, moment_part, mean_part):
    delta = global_part - mean_part
    moment_next = NESTEROV * moment_part + delta
    global_next = global_part - OUTER_RATE * (delta + NESTEROV * moment_next)
    return (global_next, moment_next)


def dot_nn(a, b):
    return jnp.dot(a, b, preferred_element_type=F32)


def dot_nt(a, b):
    return lax.dot_general(a, b, (((1,), (1,)), ((), ())), preferred_element_type=F32)


def chunk(i, size):
    return pl.ds(pl.multiple_of(i * size, size), size)


def kernel(
    step_in, hid_in, w_in, g_in, global_in, moment_in,
    proj_out, ig_out, weights_out, global_out, moment_out,
    hid, g_own, g_far, ht, n_halves, n_far, n_rows, wg, grads, ring,
    step, back_own, back_send, back_far, p_own, p_send, p_far,
    old_global, old_moment, frags,
    ag_send, ag_recv, rs_send, rs_recv, x_send, x_recv, f_send, f_recv, local,
):
    replica = lax.axis_index("replica")
    place = lax.axis_index("fsdp")
    z, side = place // 2, lax.rem(place, 2)
    up = (replica, lax.rem(z + 1, NZ) * 2 + side)
    down = (replica, lax.rem(z + NZ - 1, NZ) * 2 + side)
    partner = (replica, z * 2 + 1 - side)
    quad = lax.rem(replica, 4)
    core_twin = (replica + 1 - 2 * lax.rem(replica, 2), place)
    lane_twin = (replica - quad + lax.rem(quad + 2, 4), place)
    columns = [(lax.rem(replica + 4 * k, 16), place) for k in range(1, 4)]
    own_rows = pl.ds(pl.multiple_of(z * ROWS, 16), ROWS)

    def half_rows(block, d):
        return pl.ds(pl.multiple_of(block * ROWS + d * SIDE, 16), SIDE)

    def ring_block(step, d):
        return lax.rem(z - step + 2 * NZ, NZ) if d == 0 else lax.rem(z + step, NZ)

    load_step = pltpu.make_async_copy(step_in, step, local.at[5])
    load_step.start()
    load_hid = pltpu.make_async_copy(hid_in, hid, local.at[0])
    load_g = pltpu.make_async_copy(g_in, g_own, local.at[1])
    load_w = pltpu.make_async_copy(w_in, wg.at[own_rows], local.at[2])
    load_global = pltpu.make_async_copy(global_in, old_global, local.at[3])
    load_moment = pltpu.make_async_copy(moment_in, old_moment, local.at[4])

    barrier = pltpu.get_barrier_semaphore()
    others = (up, down, partner, core_twin, lane_twin, *columns)
    for other in others:
        pl.semaphore_signal(barrier, inc=1, device_id=other, device_id_type=MESH)
    load_hid.start()
    load_w.start()
    load_g.start()
    load_global.start()
    load_moment.start()
    pl.semaphore_wait(barrier, len(others))

    def gather_copy(step, d, part):
        rows, cols = half_rows(ring_block(step, d), d), pl.ds(part * WIDE, WIDE)
        return pltpu.make_async_remote_copy(
            src_ref=w_in.at[pl.ds(d * SIDE, SIDE), cols] if step == 0 else wg.at[rows, cols],
            dst_ref=wg.at[rows, cols],
            send_sem=ag_send.at[d, part, step],
            recv_sem=ag_recv.at[d, part, step],
            device_id=up if d == 0 else down,
            device_id_type=MESH,
        )

    def swap(src, dst, i):
        return pltpu.make_async_remote_copy(
            src_ref=src, dst_ref=dst, send_sem=x_send.at[i], recv_sem=x_recv.at[i],
            device_id=partner, device_id_type=MESH,
        )

    def frag_copy(src, dst, i, other):
        return pltpu.make_async_remote_copy(
            src_ref=frags.at[src], dst_ref=frags.at[dst],
            send_sem=f_send.at[i], recv_sem=f_recv.at[i],
            device_id=other, device_id_type=MESH,
        )

    gathers = {}

    def gather_step(step):
        for part in range(PARTS):
            for d in range(2):
                if step > 0:
                    gathers[step - 1, d, part].wait_recv()
                if step < NZ - 1:
                    gathers[step, d, part] = gather_copy(step, d, part)
                    gathers[step, d, part].start()

    def begin_weights():
        for f in range(FRAGS):
            cols = pl.ds(f * FRAGW, FRAGW)
            keep = 1.0 - (1.0 - MIX_KEEP) * chosen[f]
            own = wg[own_rows, cols].astype(F32) - INNER_RATE * grads[own_rows, cols].astype(F32)
            old_global[:, cols] = own * keep + global_out[...] * (1.0 - keep)

    def end_weights(d, part):
        kept = pl.ds(d * SIDE, SIDE)
        for f in range(part * FRAGS // PARTS, (part + 1) * FRAGS // PARTS):
            cols = pl.ds(f * FRAGW, FRAGW)
            rate = INNER_RATE * (1.0 - (1.0 - MIX_KEEP) * chosen[f])
            last = ring[d, NZ - 2, :, cols].astype(F32)
            weights_out[kept, cols] = (old_global[kept, cols] - rate * last).astype(BF16)

    sums = {}

    def sum_step(step):
        for part in range(PARTS):
            cols = pl.ds(part * WIDE, WIDE)
            for d in range(2):
                block = ring_block(step + 1, d)
                rows = half_rows(block, d)
                if step == 0:
                    src = grads.at[rows, cols]
                else:
                    sums[step - 1, d, part].wait_recv()
                    if step == NZ - 1:
                        end_weights(d, part)
                        continue
                    slot = ring.at[d, step - 1, :, cols]
                    total = grads[rows, cols].astype(F32) + slot[...].astype(F32)
                    slot[...] = total.astype(BF16)
                    src = slot
                sums[step, d, part] = pltpu.make_async_remote_copy(
                    src_ref=src,
                    dst_ref=ring.at[d, step, :, cols],
                    send_sem=rs_send.at[d, part, step],
                    recv_sem=rs_recv.at[d, part, step],
                    device_id=up if d == 0 else down,
                    device_id_type=MESH,
                )
                sums[step, d, part].start()

    gather_step(0)
    send_g = swap(g_in, g_far, 0)
    send_g.start()

    load_hid.wait()

    def turn(i, squares):
        tile = hid[:, chunk(i, 256)].astype(F32).T
        ht[chunk(i, 256), :] = tile.astype(BF16)
        return squares + jnp.sum(tile * tile, 0, keepdims=True)

    squares = lax.fori_loop(0, DW // 256, turn, jnp.zeros((1, TOK), F32))
    inverse = 1.0 / jnp.sqrt(squares * (1.0 / DW) + EPSILON)

    def normalise(i, _):
        for d in range(2):
            rows = pl.ds(pl.multiple_of((2 * i + d) * ROWS, 16), ROWS)
            n_halves[d, pl.ds(pl.multiple_of(i * ROWS, 16), ROWS), :] = (
                ht[rows, :].astype(F32) * inverse
            ).astype(BF16)
        return 0

    lax.fori_loop(0, NZ, normalise, 0)
    send_n = swap(n_halves.at[1 - side], n_far, 1)
    send_n.start()

    load_step.wait()
    turn_now = lax.rem(step[0], FRAGS).astype(F32)
    chosen = [1.0 - jnp.minimum(jnp.abs(turn_now - f), 1.0) for f in range(FRAGS)]

    def fragment(ref, rows):
        return sum(
            ref[rows, pl.ds(f * FRAGW, FRAGW)].astype(F32) * chosen[f] for f in range(FRAGS)
        )

    load_w.wait()
    frags[0] = fragment(wg, own_rows).astype(BF16)
    sent_frags = [frag_copy(0, 1, 0, core_twin)]
    sent_frags[0].start()

    load_g.wait()
    gather_step(1)

    gather_step(2)

    sent_frags[0].wait_recv()
    frags[2] = (frags[0].astype(F32) + frags[1].astype(F32)).astype(BF16)
    sent_frags.append(frag_copy(2, 3, 1, lane_twin))
    sent_frags[1].start()
    for step in range(3, 6):
        gather_step(step)

    send_g.wait_recv()
    send_n.wait_recv()

    def gradient_tile(i, _):
        rows = chunk(i, 256)
        a, b = n_halves[side, rows, :], n_far[rows, :]
        for part in range(4):
            cols = pl.ds(part * 512, 512)
            term = dot_nn(a, g_own[:, cols]) + dot_nn(b, g_far[:, cols])
            grads[rows, cols] = (term * SCALE).astype(BF16)
        return 0

    lax.fori_loop(0, HALF // 256, gradient_tile, 0)
    gather_step(6)
    sum_step(0)

    def rows_of(i, _):
        rows = chunk(i, 256)
        n_rows[0, :, rows] = n_halves[side, rows, :].astype(F32).T.astype(BF16)
        n_rows[1, :, rows] = n_far[rows, :].astype(F32).T.astype(BF16)
        return 0

    lax.fori_loop(0, HALF // 256, rows_of, 0)
    gather_step(7)

    sent_frags[1].wait_recv()
    frags[4] = (frags[2].astype(F32) + frags[3].astype(F32)).astype(BF16)
    for k in range(3):
        sent_frags.append(frag_copy(4, 5 + k, 2 + k, columns[k]))
        sent_frags[2 + k].start()

    def back_tile(far):
        def run(i, _):
            rows = chunk(i, 256)
            if far:
                back_send[rows, :] = (dot_nt(wg[rows, :], g_far[...]) * SCALE).astype(BF16)
            else:
                back_own[rows, :] = dot_nt(wg[rows, :], g_own[...]) * SCALE
            return 0

        lax.fori_loop(0, HALF // 256, run, 0)

    def project_tile(far):
        def run(i, _):
            cols = chunk(i, 512)
            if far:
                p_send[:, cols] = (dot_nn(n_rows[1], wg[:, cols]) * SCALE).astype(BF16)
            else:
                p_own[:, cols] = dot_nn(n_rows[0], wg[:, cols]) * SCALE
            return 0

        lax.fori_loop(0, KVW // 512, run, 0)

    back_tile(True)
    send_back = swap(back_send, back_far, 2)
    send_back.start()
    sum_step(1)
    project_tile(True)
    send_p = swap(p_send, p_far, 3)
    send_p.start()
    sum_step(2)
    back_tile(False)
    sum_step(3)

    load_global.wait()
    load_moment.wait()
    for k in range(3):
        sent_frags[2 + k].wait_recv()
    mean = frags[4].astype(F32)
    for k in range(3):
        mean = mean + frags[5 + k].astype(F32)
    every = pl.ds(0, ROWS)
    global_out[...], moment_out[...] = outer_update(
        fragment(old_global, every), fragment(old_moment, every), mean * (1.0 / REPLICAS)
    )
    project_tile(False)
    sum_step(4)

    send_back.wait_recv()

    def row_pair(i):
        kept = pl.ds(pl.multiple_of(i * ROWS, 16), ROWS)
        own = pl.ds(pl.multiple_of((2 * i + side) * ROWS, 16), ROWS)
        other = pl.ds(pl.multiple_of((2 * i + 1 - side) * ROWS, 16), ROWS)
        return ((back_own[kept, :], own), (back_far[kept, :].astype(F32), other))

    def overlap(i, total):
        for back, rows in row_pair(i):
            total = total + jnp.sum(back * ht[rows, :].astype(F32), 0, keepdims=True)
        return total

    total = lax.fori_loop(0, NZ, overlap, jnp.zeros((1, TOK), F32))
    factor = total * inverse * inverse * (1.0 / DW)

    def back_norm(i, _):
        for back, rows in row_pair(i):
            ht[rows, :] = ((back - ht[rows, :].astype(F32) * factor) * inverse).astype(BF16)
        return 0

    lax.fori_loop(0, NZ, back_norm, 0)

    def turn_back(i, _):
        ig_out[:, chunk(i, 256)] = ht[chunk(i, 256), :].astype(F32).T.astype(BF16)
        return 0

    lax.fori_loop(0, DW // 256, turn_back, 0)
    sum_step(5)

    send_p.wait_recv()

    def finish(i, _):
        cols = chunk(i, 512)
        proj_out[:, cols] = (p_own[:, cols] + p_far[:, cols].astype(F32)).astype(BF16)
        return 0

    lax.fori_loop(0, KVW // 512, finish, 0)
    begin_weights()
    sum_step(6)
    for copy in (send_g, send_n, send_back, send_p, *sent_frags):
        copy.wait_send()
    for copy in gathers.values():
        copy.wait_send()
    for (step, _, _), copy in sums.items():
        if step < NZ - 2:
            copy.wait_send()
    sum_step(7)

    for (step, _, _), copy in sums.items():
        if step == NZ - 2:
            copy.wait_send()


def copy_kernel(*refs):
    count = len(refs) // 2
    copies = [
        pltpu.make_async_copy(refs[i], refs[count + i], refs[-1].at[i]) for i in range(count)
    ]
    for copy in copies:
        copy.start()
    for copy in copies:
        copy.wait()


def copy_out(arrays):
    anywhere = pl.BlockSpec(memory_space=pl.ANY)
    return pl.pallas_call(
        copy_kernel,
        out_shape=tuple(jax.ShapeDtypeStruct(a.shape, a.dtype) for a in arrays),
        in_specs=[pl.BlockSpec(memory_space=pltpu.VMEM)] * len(arrays),
        out_specs=(anywhere,) * len(arrays),
        scratch_shapes=[pltpu.SemaphoreType.DMA((len(arrays),))],
        compiler_params=pltpu.CompilerParams(vmem_limit_bytes=2 << 20),
    )(*arrays)


def step_kernel(step, hidden, weights, cot, global_weights, moment):
    anywhere = pl.BlockSpec(memory_space=pl.ANY)
    vmem = pltpu.VMEM
    return pl.pallas_call(
        kernel,
        out_shape=(
            vmem((TOK, KVW), BF16),
            vmem((TOK, DW), BF16),
            vmem((ROWS, KVW), BF16),
            vmem((ROWS, FRAGW), F32),
            vmem((ROWS, FRAGW), F32),
        ),
        in_specs=[pl.BlockSpec(memory_space=pltpu.HBM)] + [anywhere] * 5,
        out_specs=(pl.BlockSpec(memory_space=pltpu.VMEM),) * 5,
        scratch_shapes=[
            vmem((TOK, DW), BF16),
            vmem((TOK, KVW), BF16),
            vmem((TOK, KVW), BF16),
            vmem((DW, TOK), BF16),
            vmem((2, HALF, TOK), BF16),
            vmem((HALF, TOK), BF16),
            vmem((2, TOK, HALF), BF16),
            vmem((HALF, KVW), BF16),
            vmem((HALF, KVW), BF16),
            vmem((2, NZ - 1, SIDE, KVW), BF16),
            pltpu.SMEM((1,), jnp.int32),
            vmem((HALF, TOK), F32),
            vmem((HALF, TOK), BF16),
            vmem((HALF, TOK), BF16),
            vmem((TOK, KVW), F32),
            vmem((TOK, KVW), BF16),
            vmem((TOK, KVW), BF16),
            vmem((ROWS, KVW), F32),
            vmem((ROWS, KVW), F32),
            vmem((8, ROWS, FRAGW), BF16),
            pltpu.SemaphoreType.DMA((2, PARTS, NZ - 1)),
            pltpu.SemaphoreType.DMA((2, PARTS, NZ - 1)),
            pltpu.SemaphoreType.DMA((2, PARTS, NZ - 1)),
            pltpu.SemaphoreType.DMA((2, PARTS, NZ - 1)),
            pltpu.SemaphoreType.DMA((4,)),
            pltpu.SemaphoreType.DMA((4,)),
            pltpu.SemaphoreType.DMA((5,)),
            pltpu.SemaphoreType.DMA((5,)),
            pltpu.SemaphoreType.DMA((6,)),
        ],
        compiler_params=pltpu.CompilerParams(
            collective_id=0, has_side_effects=True, vmem_limit_bytes=54 << 20
        ),
        cost_estimate=pl.CostEstimate(
            flops=6 * TOK * DW * KVW, bytes_accessed=600 << 20, transcendentals=0
        ),
    )(step, hidden, weights, cot, global_weights, moment)


def body(hidden_in, local_weights, cotangent, global_weights, outer_momentum, step_index):
    results = step_kernel(
        step_index, hidden_in[0], local_weights[0], cotangent[0], global_weights, outer_momentum
    )
    projected, input_grad, new_weights, new_global, new_momentum = copy_out(results)
    return (projected[None], input_grad[None], new_weights[None], new_global, new_momentum)


def solution(mesh):
    placed = (
        P("replica", "fsdp", None),
        P("replica", "fsdp", None),
        P("replica", "fsdp", None),
        P("fsdp", None),
        P("fsdp", None),
        P(),
    )
    return jax.shard_map(
        body,
        mesh=mesh,
        in_specs=placed,
        out_specs=(
            P("replica", "fsdp", None),
            P("replica", "fsdp", None),
            P("replica", "fsdp", None),
            P("fsdp", None),
            P("fsdp", None),
        ),
        check_vma=False,
    )
```

```python
import functools
import math

import jax
import jax.numpy as jnp
from jax import lax
from jax.experimental import pallas as pl
from jax.experimental.pallas import tpu as pltpu
from jax.sharding import PartitionSpec as P

KVW = 2048
FRAGS = 4
FRAGW = KVW // FRAGS
REPLICAS = 16
DW = 3584
HALF = DW // 2
TOK = 256
ROWS = 224
SIDE = ROWS // 2
NZ = 8
PARTS = 2
WIDE = KVW // PARTS
SCALE = 1.0 / math.sqrt(DW)

EPSILON = 1e-05
INNER_RATE = 0.25
OUTER_RATE = 0.7
NESTEROV = 0.9
MIX_KEEP = 0.5

MESH = pl.DeviceIdType.MESH
F32 = jnp.float32
BF16 = jnp.bfloat16


def outer_update(global_part, moment_part, mean_part):
    delta = global_part - mean_part
    moment_next = NESTEROV * moment_part + delta
    global_next = global_part - OUTER_RATE * (delta + NESTEROV * moment_next)
    return (global_next, moment_next)


def dot_nn(a, b):
    return jnp.dot(a, b, preferred_element_type=F32)


def dot_nt(a, b):
    return lax.dot_general(a, b, (((1,), (1,)), ((), ())), preferred_element_type=F32)


def chunk(i, size):
    return pl.ds(pl.multiple_of(i * size, size), size)


def kernel(
    step_in, hid_in, w_in, g_in, global_in, moment_in,
    proj_out, ig_out, weights_out, global_out, moment_out,
    hid, g_own, g_far, ht, n_halves, n_far, n_rows, wg, grads, ring,
    step, back_own, back_send, back_far, p_own, p_send, p_far,
    old_global, old_moment, frags,
    ag_send, ag_recv, rs_send, rs_recv, x_send, x_recv, f_send, f_recv, local,
):
    replica = lax.axis_index("replica")
    place = lax.axis_index("fsdp")
    z, side = place // 2, lax.rem(place, 2)
    up = (replica, lax.rem(z + 1, NZ) * 2 + side)
    down = (replica, lax.rem(z + NZ - 1, NZ) * 2 + side)
    partner = (replica, z * 2 + 1 - side)
    quad = lax.rem(replica, 4)
    core_twin = (replica + 1 - 2 * lax.rem(replica, 2), place)
    lane_twin = (replica - quad + lax.rem(quad + 2, 4), place)
    columns = [(lax.rem(replica + 4 * k, 16), place) for k in range(1, 4)]
    barrier = pltpu.get_barrier_semaphore()
    others = (up, down, partner, core_twin, lane_twin, *columns)
    for other in others:
        pl.semaphore_signal(barrier, inc=1, device_id=other, device_id_type=MESH)
    own_rows = pl.ds(pl.multiple_of(z * ROWS, 16), ROWS)

    def half_rows(block, d):
        return pl.ds(pl.multiple_of(block * ROWS + d * SIDE, 16), SIDE)

    def ring_block(step, d):
        return lax.rem(z - step + 2 * NZ, NZ) if d == 0 else lax.rem(z + step, NZ)

    load_step = pltpu.make_async_copy(step_in, step, local.at[5])
    load_hid = pltpu.make_async_copy(hid_in, hid, local.at[0])
    load_g = pltpu.make_async_copy(g_in, g_own, local.at[1])
    load_w = pltpu.make_async_copy(w_in, wg.at[own_rows], local.at[2])
    load_global = pltpu.make_async_copy(global_in, old_global, local.at[3])
    load_moment = pltpu.make_async_copy(moment_in, old_moment, local.at[4])

    load_step.start()
    load_hid.start()
    load_w.start()
    pl.semaphore_wait(barrier, len(others))

    def gather_copy(step, d, part):
        rows, cols = half_rows(ring_block(step, d), d), pl.ds(part * WIDE, WIDE)
        return pltpu.make_async_remote_copy(
            src_ref=w_in.at[pl.ds(d * SIDE, SIDE), cols] if step == 0 else wg.at[rows, cols],
            dst_ref=wg.at[rows, cols],
            send_sem=ag_send.at[d, part, step],
            recv_sem=ag_recv.at[d, part, step],
            device_id=up if d == 0 else down,
            device_id_type=MESH,
        )

    def swap(src, dst, i):
        return pltpu.make_async_remote_copy(
            src_ref=src, dst_ref=dst, send_sem=x_send.at[i], recv_sem=x_recv.at[i],
            device_id=partner, device_id_type=MESH,
        )

    def frag_copy(src, dst, i, other):
        return pltpu.make_async_remote_copy(
            src_ref=frags.at[src], dst_ref=frags.at[dst],
            send_sem=f_send.at[i], recv_sem=f_recv.at[i],
            device_id=other, device_id_type=MESH,
        )

    gathers = {}

    def gather_step(step):
        for part in range(PARTS):
            for d in range(2):
                if step > 0:
                    gathers[step - 1, d, part].wait_recv()
                if step < NZ - 1:
                    gathers[step, d, part] = gather_copy(step, d, part)
                    gathers[step, d, part].start()

    def begin_weights():
        for f in range(FRAGS):
            cols = pl.ds(f * FRAGW, FRAGW)
            keep = 1.0 - (1.0 - MIX_KEEP) * chosen[f]
            own = wg[own_rows, cols].astype(F32) - INNER_RATE * grads[own_rows, cols].astype(F32)
            old_global[:, cols] = own * keep + global_out[...] * (1.0 - keep)

    def end_weights(d, part):
        kept = pl.ds(d * SIDE, SIDE)
        for f in range(part * FRAGS // PARTS, (part + 1) * FRAGS // PARTS):
            cols = pl.ds(f * FRAGW, FRAGW)
            rate = INNER_RATE * (1.0 - (1.0 - MIX_KEEP) * chosen[f])
            last = ring[d, NZ - 2, :, cols].astype(F32)
            weights_out[kept, cols] = (old_global[kept, cols] - rate * last).astype(BF16)

    sums = {}

    def sum_step(step):
        for part in range(PARTS):
            cols = pl.ds(part * WIDE, WIDE)
            for d in range(2):
                block = ring_block(step + 1, d)
                rows = half_rows(block, d)
                if step == 0:
                    src = grads.at[rows, cols]
                else:
                    sums[step - 1, d, part].wait_recv()
                    if step == NZ - 1:
                        end_weights(d, part)
                        continue
                    slot = ring.at[d, step - 1, :, cols]
                    total = grads[rows, cols].astype(F32) + slot[...].astype(F32)
                    slot[...] = total.astype(BF16)
                    src = slot
                sums[step, d, part] = pltpu.make_async_remote_copy(
                    src_ref=src,
                    dst_ref=ring.at[d, step, :, cols],
                    send_sem=rs_send.at[d, part, step],
                    recv_sem=rs_recv.at[d, part, step],
                    device_id=up if d == 0 else down,
                    device_id_type=MESH,
                )
                sums[step, d, part].start()

    gather_step(0)
    send_g = swap(g_in, g_far, 0)
    send_g.start()
    load_g.start()
    load_global.start()
    load_moment.start()

    load_hid.wait()

    def turn(i, squares):
        tile = hid[:, chunk(i, 256)].astype(F32).T
        ht[chunk(i, 256), :] = tile.astype(BF16)
        return squares + jnp.sum(tile * tile, 0, keepdims=True)

    squares = lax.fori_loop(0, DW // 256, turn, jnp.zeros((1, TOK), F32))
    inverse = 1.0 / jnp.sqrt(squares * (1.0 / DW) + EPSILON)

    def normalise(i, _):
        for d in range(2):
            rows = pl.ds(pl.multiple_of((2 * i + d) * ROWS, 16), ROWS)
            n_halves[d, pl.ds(pl.multiple_of(i * ROWS, 16), ROWS), :] = (
                ht[rows, :].astype(F32) * inverse
            ).astype(BF16)
        return 0

    lax.fori_loop(0, NZ, normalise, 0)
    send_n = swap(n_halves.at[1 - side], n_far, 1)
    send_n.start()

    load_step.wait()
    turn_now = lax.rem(step[0], FRAGS).astype(F32)
    chosen = [1.0 - jnp.minimum(jnp.abs(turn_now - f), 1.0) for f in range(FRAGS)]

    def fragment(ref, rows):
        return sum(
            ref[rows, pl.ds(f * FRAGW, FRAGW)].astype(F32) * chosen[f] for f in range(FRAGS)
        )

    load_w.wait()
    frags[0] = fragment(wg, own_rows).astype(BF16)
    sent_frags = [frag_copy(0, 1, 0, core_twin)]
    sent_frags[0].start()

    load_g.wait()
    gather_step(1)

    gather_step(2)

    sent_frags[0].wait_recv()
    frags[2] = (frags[0].astype(F32) + frags[1].astype(F32)).astype(BF16)
    sent_frags.append(frag_copy(2, 3, 1, lane_twin))
    sent_frags[1].start()
    for step in range(3, 6):
        gather_step(step)

    send_g.wait_recv()
    send_n.wait_recv()

    def gradient_tile(i, _):
        rows = chunk(i, 256)
        a, b = n_halves[side, rows, :], n_far[rows, :]
        for part in range(4):
            cols = pl.ds(part * 512, 512)
            term = dot_nn(a, g_own[:, cols]) + dot_nn(b, g_far[:, cols])
            grads[rows, cols] = (term * SCALE).astype(BF16)
        return 0

    lax.fori_loop(0, HALF // 256, gradient_tile, 0)
    gather_step(6)
    sum_step(0)

    def rows_of(i, _):
        rows = chunk(i, 256)
        n_rows[0, :, rows] = n_halves[side, rows, :].astype(F32).T.astype(BF16)
        n_rows[1, :, rows] = n_far[rows, :].astype(F32).T.astype(BF16)
        return 0

    lax.fori_loop(0, HALF // 256, rows_of, 0)
    gather_step(7)

    sent_frags[1].wait_recv()
    frags[4] = (frags[2].astype(F32) + frags[3].astype(F32)).astype(BF16)
    for k in range(3):
        sent_frags.append(frag_copy(4, 5 + k, 2 + k, columns[k]))
        sent_frags[2 + k].start()

    def back_tile(far):
        def run(i, _):
            rows = chunk(i, 256)
            if far:
                back_send[rows, :] = (dot_nt(wg[rows, :], g_far[...]) * SCALE).astype(BF16)
            else:
                back_own[rows, :] = dot_nt(wg[rows, :], g_own[...]) * SCALE
            return 0

        lax.fori_loop(0, HALF // 256, run, 0)

    def project_tile(far):
        def run(i, _):
            cols = chunk(i, 512)
            if far:
                p_send[:, cols] = (dot_nn(n_rows[1], wg[:, cols]) * SCALE).astype(BF16)
            else:
                p_own[:, cols] = dot_nn(n_rows[0], wg[:, cols]) * SCALE
            return 0

        lax.fori_loop(0, KVW // 512, run, 0)

    back_tile(True)
    send_back = swap(back_send, back_far, 2)
    send_back.start()
    sum_step(1)
    project_tile(True)
    send_p = swap(p_send, p_far, 3)
    send_p.start()
    sum_step(2)
    back_tile(False)
    sum_step(3)

    load_global.wait()
    load_moment.wait()
    for k in range(3):
        sent_frags[2 + k].wait_recv()
    mean = frags[4].astype(F32)
    for k in range(3):
        mean = mean + frags[5 + k].astype(F32)
    every = pl.ds(0, ROWS)
    global_out[...], moment_out[...] = outer_update(
        fragment(old_global, every), fragment(old_moment, every), mean * (1.0 / REPLICAS)
    )
    project_tile(False)
    sum_step(4)

    send_back.wait_recv()

    def row_pair(i):
        kept = pl.ds(pl.multiple_of(i * ROWS, 16), ROWS)
        own = pl.ds(pl.multiple_of((2 * i + side) * ROWS, 16), ROWS)
        other = pl.ds(pl.multiple_of((2 * i + 1 - side) * ROWS, 16), ROWS)
        return ((back_own[kept, :], own), (back_far[kept, :].astype(F32), other))

    def overlap(i, total):
        for back, rows in row_pair(i):
            total = total + jnp.sum(back * ht[rows, :].astype(F32), 0, keepdims=True)
        return total

    total = lax.fori_loop(0, NZ, overlap, jnp.zeros((1, TOK), F32))
    factor = total * inverse * inverse * (1.0 / DW)

    def back_norm(i, _):
        for back, rows in row_pair(i):
            ht[rows, :] = ((back - ht[rows, :].astype(F32) * factor) * inverse).astype(BF16)
        return 0

    lax.fori_loop(0, NZ, back_norm, 0)

    def turn_back(i, _):
        ig_out[:, chunk(i, 256)] = ht[chunk(i, 256), :].astype(F32).T.astype(BF16)
        return 0

    lax.fori_loop(0, DW // 256, turn_back, 0)
    sum_step(5)

    send_p.wait_recv()

    def finish(i, _):
        cols = chunk(i, 512)
        proj_out[:, cols] = (p_own[:, cols] + p_far[:, cols].astype(F32)).astype(BF16)
        return 0

    lax.fori_loop(0, KVW // 512, finish, 0)
    begin_weights()
    sum_step(6)
    for copy in (send_g, send_n, send_back, send_p, *sent_frags):
        copy.wait_send()
    for copy in gathers.values():
        copy.wait_send()
    for (step, _, _), copy in sums.items():
        if step < NZ - 2:
            copy.wait_send()
    sum_step(7)

    for (step, _, _), copy in sums.items():
        if step == NZ - 2:
            copy.wait_send()


def copy_kernel(*refs):
    count = len(refs) // 2
    copies = [
        pltpu.make_async_copy(refs[i], refs[count + i], refs[-1].at[i]) for i in range(count)
    ]
    for i in (1, 0, 2, 3, 4):
        copies[i].start()
    for copy in copies:
        copy.wait()


def copy_out(arrays):
    anywhere = pl.BlockSpec(memory_space=pl.ANY)
    return pl.pallas_call(
        copy_kernel,
        out_shape=tuple(jax.ShapeDtypeStruct(a.shape, a.dtype) for a in arrays),
        in_specs=[pl.BlockSpec(memory_space=pltpu.VMEM)] * len(arrays),
        out_specs=(anywhere,) * len(arrays),
        scratch_shapes=[pltpu.SemaphoreType.DMA((len(arrays),))],
        compiler_params=pltpu.CompilerParams(vmem_limit_bytes=2 << 20),
    )(*arrays)


def step_kernel(step, hidden, weights, cot, global_weights, moment):
    anywhere = pl.BlockSpec(memory_space=pl.ANY)
    vmem = pltpu.VMEM
    return pl.pallas_call(
        kernel,
        out_shape=(
            vmem((TOK, KVW), BF16),
            vmem((TOK, DW), BF16),
            vmem((ROWS, KVW), BF16),
            vmem((ROWS, FRAGW), F32),
            vmem((ROWS, FRAGW), F32),
        ),
        in_specs=[pl.BlockSpec(memory_space=pltpu.HBM)] + [anywhere] * 5,
        out_specs=(pl.BlockSpec(memory_space=pltpu.VMEM),) * 5,
        scratch_shapes=[
            vmem((TOK, DW), BF16),
            vmem((TOK, KVW), BF16),
            vmem((TOK, KVW), BF16),
            vmem((DW, TOK), BF16),
            vmem((2, HALF, TOK), BF16),
            vmem((HALF, TOK), BF16),
            vmem((2, TOK, HALF), BF16),
            vmem((HALF, KVW), BF16),
            vmem((HALF, KVW), BF16),
            vmem((2, NZ - 1, SIDE, KVW), BF16),
            pltpu.SMEM((1,), jnp.int32),
            vmem((HALF, TOK), F32),
            vmem((HALF, TOK), BF16),
            vmem((HALF, TOK), BF16),
            vmem((TOK, KVW), F32),
            vmem((TOK, KVW), BF16),
            vmem((TOK, KVW), BF16),
            vmem((ROWS, KVW), F32),
            vmem((ROWS, KVW), F32),
            vmem((8, ROWS, FRAGW), BF16),
            pltpu.SemaphoreType.DMA((2, PARTS, NZ - 1)),
            pltpu.SemaphoreType.DMA((2, PARTS, NZ - 1)),
            pltpu.SemaphoreType.DMA((2, PARTS, NZ - 1)),
            pltpu.SemaphoreType.DMA((2, PARTS, NZ - 1)),
            pltpu.SemaphoreType.DMA((4,)),
            pltpu.SemaphoreType.DMA((4,)),
            pltpu.SemaphoreType.DMA((5,)),
            pltpu.SemaphoreType.DMA((5,)),
            pltpu.SemaphoreType.DMA((6,)),
        ],
        compiler_params=pltpu.CompilerParams(
            collective_id=0, has_side_effects=True, vmem_limit_bytes=54 << 20
        ),
        cost_estimate=pl.CostEstimate(
            flops=6 * TOK * DW * KVW, bytes_accessed=600 << 20, transcendentals=0
        ),
    )(step, hidden, weights, cot, global_weights, moment)


def body(hidden_in, local_weights, cotangent, global_weights, outer_momentum, step_index):
    results = step_kernel(
        step_index, hidden_in[0], local_weights[0], cotangent[0], global_weights, outer_momentum
    )
    projected, input_grad, new_weights, new_global, new_momentum = copy_out(results)
    return (projected[None], input_grad[None], new_weights[None], new_global, new_momentum)


def solution(mesh):
    placed = (
        P("replica", "fsdp", None),
        P("replica", "fsdp", None),
        P("replica", "fsdp", None),
        P("fsdp", None),
        P("fsdp", None),
        P(),
    )
    return jax.shard_map(
        body,
        mesh=mesh,
        in_specs=placed,
        out_specs=(
            P("replica", "fsdp", None),
            P("replica", "fsdp", None),
            P("replica", "fsdp", None),
            P("fsdp", None),
            P("fsdp", None),
        ),
        check_vma=False,
    )
```

```python
import functools
import math

import jax
import jax.numpy as jnp
from jax import lax
from jax.experimental import pallas as pl
from jax.experimental.pallas import tpu as pltpu
from jax.sharding import PartitionSpec as P

KVW = 2048
FRAGS = 4
FRAGW = KVW // FRAGS
REPLICAS = 16
DW = 3584
HALF = DW // 2
TOK = 256
ROWS = 224
SIDE = ROWS // 2
NZ = 8
HOPS = NZ // 2
PARTS = 2
WIDE = KVW // PARTS
SCALE = 1.0 / math.sqrt(DW)

EPSILON = 1e-05
INNER_RATE = 0.25
OUTER_RATE = 0.7
NESTEROV = 0.9
MIX_KEEP = 0.5

MESH = pl.DeviceIdType.MESH
F32 = jnp.float32
BF16 = jnp.bfloat16


def outer_update(global_part, moment_part, mean_part):
    delta = global_part - mean_part
    moment_next = NESTEROV * moment_part + delta
    global_next = global_part - OUTER_RATE * (delta + NESTEROV * moment_next)
    return (global_next, moment_next)


def dot_nn(a, b):
    return jnp.dot(a, b, preferred_element_type=F32)


def dot_nt(a, b):
    return lax.dot_general(a, b, (((1,), (1,)), ((), ())), preferred_element_type=F32)


def chunk(i, size):
    return pl.ds(pl.multiple_of(i * size, size), size)


def kernel(
    step_in, hid_in, w_in, g_in, global_in, moment_in,
    proj_out, ig_out, weights_out, global_out, moment_out,
    hid, g_own, g_far, ht, n_halves, n_far, n_rows, wg, grads, ring,
    step, back_own, back_send, back_far, p_own, p_send, p_far,
    old_global, old_moment, frags,
    ag_send, ag_recv, rs_send, rs_recv, x_send, x_recv, f_send, f_recv, local,
):
    replica = lax.axis_index("replica")
    place = lax.axis_index("fsdp")
    z, side = place // 2, lax.rem(place, 2)
    up = (replica, lax.rem(z + 1, NZ) * 2 + side)
    down = (replica, lax.rem(z + NZ - 1, NZ) * 2 + side)
    partner = (replica, z * 2 + 1 - side)
    quad = lax.rem(replica, 4)
    core_twin = (replica + 1 - 2 * lax.rem(replica, 2), place)
    lane_twin = (replica - quad + lax.rem(quad + 2, 4), place)
    columns = [(lax.rem(replica + 4 * k, 16), place) for k in range(1, 4)]
    barrier = pltpu.get_barrier_semaphore()
    others = (up, down, partner, core_twin, lane_twin, *columns)
    for other in others:
        pl.semaphore_signal(barrier, inc=1, device_id=other, device_id_type=MESH)
    own_rows = pl.ds(pl.multiple_of(z * ROWS, 16), ROWS)

    def half_rows(block, d):
        return pl.ds(pl.multiple_of(block * ROWS + d * SIDE, 16), SIDE)

    def ring_block(step, d):
        return lax.rem(z - step + 2 * NZ, NZ) if d == 0 else lax.rem(z + step, NZ)

    load_step = pltpu.make_async_copy(step_in, step, local.at[5])
    load_hid = pltpu.make_async_copy(hid_in, hid, local.at[0])
    load_g = pltpu.make_async_copy(g_in, g_own, local.at[1])
    load_w = pltpu.make_async_copy(w_in, wg.at[own_rows], local.at[2])
    load_global = pltpu.make_async_copy(global_in, old_global, local.at[3])
    load_moment = pltpu.make_async_copy(moment_in, old_moment, local.at[4])

    load_step.start()
    load_hid.start()
    load_w.start()
    pl.semaphore_wait(barrier, len(others))

    def chunks(step, d, last):
        for half in (d, 1 - d):
            if step == last and half != d:
                continue
            for part in range(PARTS):
                yield half, part, pl.ds(part * WIDE, WIDE)

    def gather_copy(step, d, half, part):
        rows, cols = half_rows(ring_block(step, d), half), pl.ds(part * WIDE, WIDE)
        return pltpu.make_async_remote_copy(
            src_ref=w_in.at[pl.ds(half * SIDE, SIDE), cols] if step == 0 else wg.at[rows, cols],
            dst_ref=wg.at[rows, cols],
            send_sem=ag_send.at[d, half, part, step],
            recv_sem=ag_recv.at[d, half, part, step],
            device_id=up if d == 0 else down,
            device_id_type=MESH,
        )

    def swap(src, dst, i):
        return pltpu.make_async_remote_copy(
            src_ref=src, dst_ref=dst, send_sem=x_send.at[i], recv_sem=x_recv.at[i],
            device_id=partner, device_id_type=MESH,
        )

    def frag_copy(src, dst, i, other):
        return pltpu.make_async_remote_copy(
            src_ref=frags.at[src], dst_ref=frags.at[dst],
            send_sem=f_send.at[i], recv_sem=f_recv.at[i],
            device_id=other, device_id_type=MESH,
        )

    gathers = {}

    def gather_step(step):
        for k in range(2 * PARTS):
            for d in range(2):
                if step > 0:
                    arrived = list(chunks(step - 1, d, HOPS - 1))
                    if k < len(arrived):
                        half, part, _ = arrived[k]
                        gathers[step - 1, d, half, part].wait_recv()
                leaving = list(chunks(step, d, HOPS - 1)) if step < HOPS else []
                if k < len(leaving):
                    half, part, _ = leaving[k]
                    gathers[step, d, half, part] = gather_copy(step, d, half, part)
                    gathers[step, d, half, part].start()

    def begin_weights():
        for f in range(FRAGS):
            cols = pl.ds(f * FRAGW, FRAGW)
            keep = 1.0 - (1.0 - MIX_KEEP) * chosen[f]
            own = wg[own_rows, cols].astype(F32) - INNER_RATE * grads[own_rows, cols].astype(F32)
            old_global[:, cols] = own * keep + global_out[...] * (1.0 - keep)

    sums = {}

    def sum_send(step, d, half, part, cols, src):
        sums[step, d, half, part] = pltpu.make_async_remote_copy(
            src_ref=src,
            dst_ref=ring.at[d, step, half, :, cols],
            send_sem=rs_send.at[d, half, part, step],
            recv_sem=rs_recv.at[d, half, part, step],
            device_id=up if d == 0 else down,
            device_id_type=MESH,
        )
        sums[step, d, half, part].start()

    def sum_step(step):
        for k in range(2 * PARTS):
            for d in range(2):
                todo = list(chunks(step, d, 0))
                if k >= len(todo):
                    continue
                half, part, cols = todo[k]
                rows = half_rows(ring_block(step + HOPS, d), half)
                if (step - 1, d, half, part) in sums:
                    sums[step - 1, d, half, part].wait_recv()
                    slot = ring.at[d, step - 1, half, :, cols]
                    total = grads[rows, cols].astype(F32) + slot[...].astype(F32)
                    slot[...] = total.astype(BF16)
                    sum_send(step, d, half, part, cols, slot)
                else:
                    sum_send(step, d, half, part, cols, grads.at[rows, cols])

    def sum_end():
        last = HOPS - 1
        for k in range(2 * PARTS):
            half, part = k % 2, k // 2
            for d in (half, 1 - half):
                sums[last, d, half, part].wait_recv()
            kept = pl.ds(half * SIDE, SIDE)
            for f in range(part * FRAGS // PARTS, (part + 1) * FRAGS // PARTS):
                cols = pl.ds(f * FRAGW, FRAGW)
                rate = INNER_RATE * (1.0 - (1.0 - MIX_KEEP) * chosen[f])
                total = ring[0, last, half, :, cols].astype(F32) + ring[1, last, half, :, cols].astype(F32)
                weights_out[kept, cols] = (old_global[kept, cols] - rate * total).astype(BF16)

    gather_step(0)
    send_g = swap(g_in, g_far, 0)
    send_g.start()
    load_g.start()
    load_global.start()
    load_moment.start()

    load_hid.wait()

    def turn(i, squares):
        tile = hid[:, chunk(i, 256)].astype(F32).T
        ht[chunk(i, 256), :] = tile.astype(BF16)
        return squares + jnp.sum(tile * tile, 0, keepdims=True)

    squares = lax.fori_loop(0, DW // 256, turn, jnp.zeros((1, TOK), F32))
    inverse = 1.0 / jnp.sqrt(squares * (1.0 / DW) + EPSILON)

    def normalise(i, _):
        for d in range(2):
            rows = pl.ds(pl.multiple_of((2 * i + d) * ROWS, 16), ROWS)
            n_halves[d, pl.ds(pl.multiple_of(i * ROWS, 16), ROWS), :] = (
                ht[rows, :].astype(F32) * inverse
            ).astype(BF16)
        return 0

    lax.fori_loop(0, NZ, normalise, 0)
    send_n = swap(n_halves.at[1 - side], n_far, 1)
    send_n.start()

    load_step.wait()
    turn_now = lax.rem(step[0], FRAGS).astype(F32)
    chosen = [1.0 - jnp.minimum(jnp.abs(turn_now - f), 1.0) for f in range(FRAGS)]

    def fragment(ref, rows):
        return sum(
            ref[rows, pl.ds(f * FRAGW, FRAGW)].astype(F32) * chosen[f] for f in range(FRAGS)
        )

    load_w.wait()
    frags[0] = fragment(wg, own_rows).astype(BF16)
    sent_frags = [frag_copy(0, 1, 0, core_twin)]
    sent_frags[0].start()

    load_g.wait()
    gather_step(1)

    sent_frags[0].wait_recv()
    frags[2] = (frags[0].astype(F32) + frags[1].astype(F32)).astype(BF16)
    sent_frags.append(frag_copy(2, 3, 1, lane_twin))
    sent_frags[1].start()
    gather_step(2)

    send_g.wait_recv()
    send_n.wait_recv()

    def gradient_tile(i, _):
        rows = chunk(i, 256)
        a, b = n_halves[side, rows, :], n_far[rows, :]
        for part in range(4):
            cols = pl.ds(part * 512, 512)
            term = dot_nn(a, g_own[:, cols]) + dot_nn(b, g_far[:, cols])
            grads[rows, cols] = (term * SCALE).astype(BF16)
        return 0

    lax.fori_loop(0, HALF // 256, gradient_tile, 0)
    gather_step(3)
    sum_step(0)

    def rows_of(i, _):
        rows = chunk(i, 256)
        n_rows[0, :, rows] = n_halves[side, rows, :].astype(F32).T.astype(BF16)
        n_rows[1, :, rows] = n_far[rows, :].astype(F32).T.astype(BF16)
        return 0

    lax.fori_loop(0, HALF // 256, rows_of, 0)
    gather_step(4)

    sent_frags[1].wait_recv()
    frags[4] = (frags[2].astype(F32) + frags[3].astype(F32)).astype(BF16)
    for k in range(3):
        sent_frags.append(frag_copy(4, 5 + k, 2 + k, columns[k]))
        sent_frags[2 + k].start()

    def back_tile(far):
        def run(i, _):
            rows = chunk(i, 256)
            if far:
                back_send[rows, :] = (dot_nt(wg[rows, :], g_far[...]) * SCALE).astype(BF16)
            else:
                back_own[rows, :] = dot_nt(wg[rows, :], g_own[...]) * SCALE
            return 0

        lax.fori_loop(0, HALF // 256, run, 0)

    def project_tile(far):
        def run(i, _):
            cols = chunk(i, 512)
            if far:
                p_send[:, cols] = (dot_nn(n_rows[1], wg[:, cols]) * SCALE).astype(BF16)
            else:
                p_own[:, cols] = dot_nn(n_rows[0], wg[:, cols]) * SCALE
            return 0

        lax.fori_loop(0, KVW // 512, run, 0)

    back_tile(True)
    send_back = swap(back_send, back_far, 2)
    send_back.start()
    project_tile(True)
    send_p = swap(p_send, p_far, 3)
    send_p.start()
    sum_step(1)
    back_tile(False)
    project_tile(False)

    load_global.wait()
    load_moment.wait()
    for k in range(3):
        sent_frags[2 + k].wait_recv()
    mean = frags[4].astype(F32)
    for k in range(3):
        mean = mean + frags[5 + k].astype(F32)
    every = pl.ds(0, ROWS)
    global_out[...], moment_out[...] = outer_update(
        fragment(old_global, every), fragment(old_moment, every), mean * (1.0 / REPLICAS)
    )
    project_tile(False)
    sum_step(2)

    send_back.wait_recv()

    def row_pair(i):
        kept = pl.ds(pl.multiple_of(i * ROWS, 16), ROWS)
        own = pl.ds(pl.multiple_of((2 * i + side) * ROWS, 16), ROWS)
        other = pl.ds(pl.multiple_of((2 * i + 1 - side) * ROWS, 16), ROWS)
        return ((back_own[kept, :], own), (back_far[kept, :].astype(F32), other))

    def overlap(i, total):
        for back, rows in row_pair(i):
            total = total + jnp.sum(back * ht[rows, :].astype(F32), 0, keepdims=True)
        return total

    total = lax.fori_loop(0, NZ, overlap, jnp.zeros((1, TOK), F32))
    factor = total * inverse * inverse * (1.0 / DW)

    def back_norm(i, _):
        for back, rows in row_pair(i):
            ht[rows, :] = ((back - ht[rows, :].astype(F32) * factor) * inverse).astype(BF16)
        return 0

    lax.fori_loop(0, NZ, back_norm, 0)

    def turn_back(i, _):
        ig_out[:, chunk(i, 256)] = ht[chunk(i, 256), :].astype(F32).T.astype(BF16)
        return 0

    lax.fori_loop(0, DW // 256, turn_back, 0)
    sum_step(3)

    send_p.wait_recv()

    def finish(i, _):
        cols = chunk(i, 512)
        proj_out[:, cols] = (p_own[:, cols] + p_far[:, cols].astype(F32)).astype(BF16)
        return 0

    lax.fori_loop(0, KVW // 512, finish, 0)
    begin_weights()
    for copy in (send_g, send_n, send_back, send_p, *sent_frags):
        copy.wait_send()
    for copy in gathers.values():
        copy.wait_send()
    for (step, _, _, _), copy in sums.items():
        if step < HOPS - 1:
            copy.wait_send()
    sum_end()
    for (step, _, _, _), copy in sums.items():
        if step == HOPS - 1:
            copy.wait_send()


def copy_kernel(*refs):
    count = len(refs) // 2
    copies = [
        pltpu.make_async_copy(refs[i], refs[count + i], refs[-1].at[i]) for i in range(count)
    ]
    for i in (1, 0, 2, 3, 4):
        copies[i].start()
    for copy in copies:
        copy.wait()


def copy_out(arrays):
    anywhere = pl.BlockSpec(memory_space=pl.ANY)
    return pl.pallas_call(
        copy_kernel,
        out_shape=tuple(jax.ShapeDtypeStruct(a.shape, a.dtype) for a in arrays),
        in_specs=[pl.BlockSpec(memory_space=pltpu.VMEM)] * len(arrays),
        out_specs=(anywhere,) * len(arrays),
        scratch_shapes=[pltpu.SemaphoreType.DMA((len(arrays),))],
        compiler_params=pltpu.CompilerParams(vmem_limit_bytes=2 << 20),
    )(*arrays)


def step_kernel(step, hidden, weights, cot, global_weights, moment):
    anywhere = pl.BlockSpec(memory_space=pl.ANY)
    vmem = pltpu.VMEM
    return pl.pallas_call(
        kernel,
        out_shape=(
            vmem((TOK, KVW), BF16),
            vmem((TOK, DW), BF16),
            vmem((ROWS, KVW), BF16),
            vmem((ROWS, FRAGW), F32),
            vmem((ROWS, FRAGW), F32),
        ),
        in_specs=[pl.BlockSpec(memory_space=pltpu.HBM)] + [anywhere] * 5,
        out_specs=(pl.BlockSpec(memory_space=pltpu.VMEM),) * 5,
        scratch_shapes=[
            vmem((TOK, DW), BF16),
            vmem((TOK, KVW), BF16),
            vmem((TOK, KVW), BF16),
            vmem((DW, TOK), BF16),
            vmem((2, HALF, TOK), BF16),
            vmem((HALF, TOK), BF16),
            vmem((2, TOK, HALF), BF16),
            vmem((HALF, KVW), BF16),
            vmem((HALF, KVW), BF16),
            vmem((2, HOPS, 2, SIDE, KVW), BF16),
            pltpu.SMEM((1,), jnp.int32),
            vmem((HALF, TOK), F32),
            vmem((HALF, TOK), BF16),
            vmem((HALF, TOK), BF16),
            vmem((TOK, KVW), F32),
            vmem((TOK, KVW), BF16),
            vmem((TOK, KVW), BF16),
            vmem((ROWS, KVW), F32),
            vmem((ROWS, KVW), F32),
            vmem((8, ROWS, FRAGW), BF16),
            pltpu.SemaphoreType.DMA((2, 2, PARTS, HOPS)),
            pltpu.SemaphoreType.DMA((2, 2, PARTS, HOPS)),
            pltpu.SemaphoreType.DMA((2, 2, PARTS, HOPS)),
            pltpu.SemaphoreType.DMA((2, 2, PARTS, HOPS)),
            pltpu.SemaphoreType.DMA((4,)),
            pltpu.SemaphoreType.DMA((4,)),
            pltpu.SemaphoreType.DMA((5,)),
            pltpu.SemaphoreType.DMA((5,)),
            pltpu.SemaphoreType.DMA((6,)),
        ],
        compiler_params=pltpu.CompilerParams(
            collective_id=0, has_side_effects=True, vmem_limit_bytes=55 << 20
        ),
        cost_estimate=pl.CostEstimate(
            flops=6 * TOK * DW * KVW, bytes_accessed=600 << 20, transcendentals=0
        ),
    )(step, hidden, weights, cot, global_weights, moment)


def body(hidden_in, local_weights, cotangent, global_weights, outer_momentum, step_index):
    results = step_kernel(
        step_index, hidden_in[0], local_weights[0], cotangent[0], global_weights, outer_momentum
    )
    projected, input_grad, new_weights, new_global, new_momentum = copy_out(results)
    return (projected[None], input_grad[None], new_weights[None], new_global, new_momentum)


def solution(mesh):
    placed = (
        P("replica", "fsdp", None),
        P("replica", "fsdp", None),
        P("replica", "fsdp", None),
        P("fsdp", None),
        P("fsdp", None),
        P(),
    )
    return jax.shard_map(
        body,
        mesh=mesh,
        in_specs=placed,
        out_specs=(
            P("replica", "fsdp", None),
            P("replica", "fsdp", None),
            P("replica", "fsdp", None),
            P("fsdp", None),
            P("fsdp", None),
        ),
        check_vma=False,
    )
```
